256 devices in a mesh: gx: 8 (over x, z_hi), gy: 8 (over y, core), gz: 4 (over z_lo).
Axes of the slice: x: 4, y: 4, z: 8 (z_hi: 2, z_lo: 4; z = z_hi * 4 + z_lo), core: 2. Of those that a mesh axis runs over, the one named last changes fastest.
Arguments:
- adjoint_source: bfloat16 [32, 32, 8, 175, 128], P('gx', 'gy', 'gz'), may hold values from -6 to 6
- warm_start: bfloat16 [32, 32, 8, 175, 128], P('gx', 'gy', 'gz'), may hold values from -6 to 6
- block_inverse: bfloat16 [32, 32, 8, 175, 175], P('gx', 'gy', 'gz'), may hold values from -2 to 2
- face_jacobian: bfloat16 [32, 32, 8, 6, 75, 75], P('gx', 'gy', 'gz'), may hold values from -0.4375 to 0.4375
- trace_basis: bfloat16 [6, 175, 75], replicated, may hold values from -0.4375 to 0.4375
- orientation: int32 [32, 32, 8, 6, 15], P('gx', 'gy', 'gz'), may hold values from 0 to 14, each once within a row
Outputs:
- adjoint: bfloat16 [32, 32, 8, 175, 128], P('gx', 'gy', 'gz')
- shape_gradient: float32 [32, 32, 8, 6, 128], P('gx', 'gy', 'gz')
The draws below stay inside these ranges and needn't reach their ends.
Inputs may be any that keep to these rules, and one draw needn't show every extreme that they name: `orientation`: every row of 15 entries is a permutation of 0 to 14.
All inputs are finite; a program needn't handle non-finite values.
Results may differ from the reference program's by a relative error of at most 0.011.
Values may be sent and summed in bfloat16 or wider, within the bound.
No kernel may reach another device: no remote copies, remote signals or barrier semaphores. Data moves between devices by JAX's collectives and lax.ppermute only.
A program may use at most 128 MiB of HBM per device.

```python
import math
import jax
import jax.numpy as jnp
from jax import lax

VARS = 5
FMODES = 15
R = 128
SWEEPS = 2
C = 175
TR = 75
NX = 32
NY = 32
NZ = 8


def draw_block_inverse(key, part):
    key = jax.random.fold_in(key, 11)
    noise_key, scale_key = jax.random.split(key)
    shape = (NX, NY, NZ, C, C)
    identity = jnp.eye(C, dtype=jnp.float32)
    noise = jnp.clip(jax.random.normal(noise_key, shape, jnp.float32), -6.0, 6.0)
    row_scale = jax.random.uniform(scale_key, (NX, NY, NZ, C, 1), jnp.float32, 0.8, 1.25)
    blocks = (identity + 0.5 * noise / math.sqrt(C)) * row_scale
    return blocks.astype(jnp.bfloat16)


def levels(rng, dims, cuts, least, top_value):
    def one(axis_at, shards_of):
        steps = jax.random.uniform(jax.random.fold_in(jax.random.fold_in(rng, 6), axis_at), (shards_of,), jnp.float32, least / len(cuts), top_value / len(cuts))
        return jnp.repeat(jnp.exp(steps), dims[axis_at] // shards_of).reshape((-1,) + (1,) * (len(dims) - axis_at - 1))

    gain = one(*cuts[0])
    for cut in cuts[1:]:
        gain = gain * one(*cut)
    return gain


def normal_values(key, extent, scale, bound, cuts=(), held_as=jnp.bfloat16):
    result = scale * jax.random.normal(key, extent, jnp.float32)
    if cuts:
        result = result * levels(key, extent, cuts, -0.22, 0.18)
    return jnp.clip(result, -bound, bound).astype(held_as)


def setup_inputs(seed: int = 0) -> dict:
    streams_of = jax.random.split(jax.random.key(seed), 7)
    adjoint_source = normal_values(streams_of[0], (NX, NY, NZ, C, R), 1.0, 6.0, ((0, 8), (1, 8), (2, 4)))
    warm_start = normal_values(streams_of[1], (NX, NY, NZ, C, R), 1.0, 6.0, ((0, 8), (1, 8), (2, 4)))
    block_inverse = draw_block_inverse(jax.random.fold_in(streams_of[6], 71), 0)
    face_jacobian = normal_values(streams_of[3], (NX, NY, NZ, 6, TR, TR), (0.25 / TR ** 0.5), 0.4375, ((0, 8), (1, 8), (2, 4)))
    trace_basis = normal_values(streams_of[4], (6, C, TR), C ** -0.5, 0.4375)
    orientation = jax.vmap(lambda own: jax.random.permutation(own, FMODES))(jax.random.split(streams_of[5], NX * NY * NZ * 6)).reshape((NX, NY, NZ, 6, FMODES)).astype(jnp.int32)
    return dict(adjoint_source=adjoint_source, warm_start=warm_start, block_inverse=block_inverse, face_jacobian=face_jacobian, trace_basis=trace_basis, orientation=orientation)


def orient_index(orientation):
    modes = orientation.shape[-1]
    base = jnp.arange(VARS, dtype=jnp.int32)[:, None] * modes
    full_index = base + orientation[..., None, :]
    return full_index.reshape(orientation.shape[:-1] + (VARS * modes,)).astype(jnp.int32)


def permuter(index_slab):
    width = index_slab.shape[-1]
    return (index_slab[..., :, None] == jnp.arange(width, dtype=jnp.int32)).astype(jnp.float32)


def face_traces(adjoint, trace_basis):
    basis = trace_basis.astype(jnp.float32)

    def per_slab(slab):
        return jnp.einsum('fck,yzcr->yzfkr', basis, slab.astype(jnp.float32)).astype(jnp.bfloat16)

    return lax.map(per_slab, adjoint)


def neighbor_traces(traces):
    empty_plane = jnp.zeros_like(traces[:, :, :1, 0])
    west_side = jnp.roll(traces[:, :, :, 1], 1, axis=0)
    east_side = jnp.roll(traces[:, :, :, 0], -1, axis=0)
    south_side = jnp.roll(traces[:, :, :, 3], 1, axis=1)
    north_side = jnp.roll(traces[:, :, :, 2], -1, axis=1)
    bottom_side = jnp.concatenate([empty_plane, traces[:, :, :-1, 5]], axis=2)
    top_side = jnp.concatenate([traces[:, :, 1:, 4], empty_plane], axis=2)
    return jnp.stack([west_side, east_side, south_side, north_side, bottom_side, top_side], axis=3)


def aligned_flux(near_slab, index_slab, jacobian_slab):
    aligned = jnp.einsum('yzfij,yzfjr->yzfir', permuter(index_slab), near_slab.astype(jnp.float32))
    flux = jnp.einsum('yzfki,yzfir->yzfkr', jacobian_slab.astype(jnp.float32), aligned)
    return aligned, flux


def sweep_once(adjoint, adjoint_source, block_inverse, face_jacobian, trace_basis, full_index):
    near = neighbor_traces(face_traces(adjoint, trace_basis))
    basis = trace_basis.astype(jnp.float32)

    def per_slab(args):
        near_slab, index_slab, jacobian_slab, inverse_slab, source_slab = args
        aligned, flux = aligned_flux(near_slab, index_slab, jacobian_slab)
        flux_rounded = lax.optimization_barrier(flux.astype(jnp.bfloat16))
        coupling = jnp.einsum('fck,yzfkr->yzcr', basis, flux_rounded.astype(jnp.float32))
        residual = lax.optimization_barrier((source_slab.astype(jnp.float32) - coupling).astype(jnp.bfloat16))
        updated = jnp.einsum('yzcd,yzdr->yzcr', inverse_slab.astype(jnp.float32), residual.astype(jnp.float32))
        return updated.astype(jnp.bfloat16)

    return lax.map(per_slab, (near, full_index, face_jacobian, block_inverse, adjoint_source))


def reference(adjoint_source, warm_start, block_inverse, face_jacobian, trace_basis, orientation):
    full_index = orient_index(orientation)
    adjoint = warm_start
    for iteration in range(SWEEPS):
        adjoint = sweep_once(adjoint, adjoint_source, block_inverse, face_jacobian, trace_basis, full_index)
    traces = face_traces(adjoint, trace_basis)
    near = neighbor_traces(traces)

    def per_slab(args):
        near_slab, own_slab, index_slab, jacobian_slab = args
        aligned, flux = aligned_flux(near_slab, index_slab, jacobian_slab)
        return jnp.sum((own_slab.astype(jnp.float32) - aligned) * flux, axis=3)

    shape_gradient = lax.map(per_slab, (near, traces, full_index, face_jacobian))
    return adjoint, shape_gradient
```

```python
import jax
import jax.numpy as jnp
from jax import lax
from jax.experimental import pallas as pl
from jax.experimental.pallas import tpu as pltpu
from jax.sharding import PartitionSpec as P

SWEEPS = 2
PAIR = 76
PAD = 80
LANES = 128
BF = jnp.bfloat16
F32 = jnp.float32
PARAMS = pltpu.CompilerParams(vmem_limit_bytes=40 * 1024 * 1024)
VMEM = pl.BlockSpec(memory_space=pltpu.VMEM)


def mm(a, b):
    return jnp.dot(a, b, preferred_element_type=F32)


def mm_t(a, b):
    return lax.dot_general(a, b, (((1,), (1,)), ((), ())), preferred_element_type=F32)


def call(kernel, out_shape, operands, flops, scratch=()):
    moved = sum(a.size * a.dtype.itemsize for a in operands)
    return pl.pallas_call(
        kernel,
        out_shape=out_shape,
        in_specs=[VMEM] * len(operands),
        out_specs=jax.tree.map(lambda _: VMEM, out_shape),
        scratch_shapes=list(scratch),
        compiler_params=PARAMS,
        cost_estimate=pl.CostEstimate(flops=flops, bytes_accessed=moved, transcendentals=0),
    )(*operands)


class Block:
    def __init__(self, nx, ny, nz, c, r):
        self.nx, self.ny, self.nz, self.c, self.r = nx, ny, nz, c, r
        self.plane = ny * nz

    def send_shapes(self):
        rows = self.nz * PAIR
        x = jax.ShapeDtypeStruct((self.ny, rows, self.r), BF)
        y = jax.ShapeDtypeStruct((self.nx, rows, self.r), BF)
        z = jax.ShapeDtypeStruct((self.nx * self.ny // 2, 2 * PAIR, self.r), BF)
        return [x, x, y, y, z, z]

    def slot(self, face, x, y, z):
        if face < 2:
            return (y, pl.ds(z * PAIR, PAIR))
        if face < 4:
            return (x, pl.ds(z * PAIR, PAIR))
        return (x * (self.ny // 2) + y // 2, pl.ds((y % 2) * PAIR, PAIR))

    def halo_faces(self, x_side, y, z):
        faces = [] if x_side is None else [x_side]
        if y == 0:
            faces.append(2)
        if y == self.ny - 1:
            faces.append(3)
        if z == 0:
            faces.append(4)
        if z == self.nz - 1:
            faces.append(5)
        return faces

    def work(self, x, x_side):
        return [
            (x * self.plane + y * self.nz + z, y, z, self.halo_faces(x_side, y, z))
            for y in range(self.ny)
            for z in range(self.nz)
        ]

    def planes(self, visit):
        def inner(x, carry):
            visit(x, None)
            return carry

        lax.fori_loop(1, self.nx - 1, inner, 0)
        visit(0, 0)
        visit(self.nx - 1, 1)

    def near_local(self, face, x, y, z):
        dx, dy, dz = [(-1, 0, 0), (1, 0, 0), (0, -1, 0), (0, 1, 0), (0, 0, -1), (0, 0, 1)][face]
        return (x + 1 + dx) * self.plane + (y + dy) * self.nz + (z + dz), face ^ 1


def send_traces(block, x, work, values, bt, sends):
    traces = [
        mm(jnp.concatenate([bt[f] for f in faces], axis=0), a).astype(BF)
        for (_, _, _, faces), a in zip(work, values)
    ]
    for (_, y, z, faces), t in zip(work, traces):
        for i, f in enumerate(faces):
            sends[f][block.slot(f, x, y, z)] = t[i * PAD : i * PAD + PAIR]


def first_sends(block, a, bt):
    def kernel(a_ref, bt_ref, *sends):
        def visit(x, x_side):
            work = block.work(x, x_side)
            send_traces(block, x, work, [a_ref[w[0]] for w in work], bt_ref, sends)

        block.planes(visit)

    return call(kernel, block.send_shapes(), [a, bt], 64 * 80 * 175 * 256)


def permuted(jacobian, index):
    count = jacobian.shape[0]
    group = 6

    def kernel(j_ref, i_ref, jp_ref, p_ref):
        rows = lax.broadcasted_iota(jnp.int32, (PAD, PAD), 0)
        cols = lax.broadcasted_iota(jnp.int32, (PAD, PAD), 1)
        eye = (rows == cols).astype(BF)

        def element(e, carry):
            both = []
            for f in range(group):
                transposed = (rows == i_ref[e, f : f + 1, :]).astype(BF)
                both.append(mm_t(jnp.concatenate([j_ref[e, f], eye], axis=0), transposed).astype(BF))
            for f in range(group):
                jp_ref[e, f] = both[f][:PAD]
                p_ref[e, f] = both[f][PAD:]
            return carry

        lax.fori_loop(0, count, element, 0)

    shape = jax.ShapeDtypeStruct((count, group, PAD, PAD), BF)
    return call(kernel, [shape, shape], [jacobian, index], count * 6 * 160 * 80 * 160)


def fill_traces(block, a_ref, bt_ref, t_ref):
    nx, plane = block.nx, block.plane
    t_ref[0:plane, 1] = jnp.zeros((plane, PAD, block.r), BF)
    t_ref[(nx + 1) * plane : (nx + 2) * plane, 0] = jnp.zeros((plane, PAD, block.r), BF)
    every = bt_ref[...].reshape(6 * PAD, block.c)

    def traces(x, carry):
        t = [mm(every, a_ref[x * plane + i]).astype(BF) for i in range(plane)]
        for i in range(plane):
            for f in range(6):
                t_ref[(x + 1) * plane + i, f] = t[i][f * PAD : (f + 1) * PAD]
        return carry

    lax.fori_loop(0, nx, traces, 0)


def local_faces(block, y, z):
    return [f for f in range(6) if f < 2 or f not in block.halo_faces(None, y, z)]


def widened(pieces):
    gap = jnp.zeros((LANES - PAD, pieces[0].shape[1]), BF)
    return jnp.concatenate([part for p in pieces for part in (p, gap)], axis=0)


def coupled(bc_ref, faces, fluxes):
    return mm(jnp.concatenate([bc_ref[f] for f in faces], axis=1), widened(fluxes))


def local_residual(block, a, source, jp, bt, bc):
    def kernel(a_ref, s_ref, j_ref, bt_ref, bc_ref, r_ref, t_ref):
        fill_traces(block, a_ref, bt_ref, t_ref)

        def plane(x, carry):
            work = [(e, y, z, local_faces(block, y, z)) for e, y, z, _ in block.work(x, None)]
            fluxes = [
                [mm(j_ref[e, f], t_ref[block.near_local(f, x, y, z)]).astype(BF) for f in faces]
                for e, y, z, faces in work
            ]
            rest = [
                s_ref[w[0]].astype(F32) - coupled(bc_ref, w[3], flux) for w, flux in zip(work, fluxes)
            ]
            for w, value in zip(work, rest):
                r_ref[w[0]] = value
            return carry

        lax.fori_loop(0, block.nx, plane, 0)

    count = block.nx * block.plane
    return call(
        kernel,
        jax.ShapeDtypeStruct((count, block.c, block.r), F32),
        [a, source, jp, bt, bc],
        count * 175 * 480 * 128 * 4,
        [pltpu.VMEM(((block.nx + 2) * block.plane, 6, PAD, block.r), BF)],
    )


def finish_sweep(block, halos, residual, inverse, jp, bt, bc):
    def kernel(*refs):
        near, (r_ref, v_ref, j_ref, bt_ref, bc_ref, a_ref), sends = refs[:6], refs[6:12], refs[12:]

        def visit(x, x_side):
            work = block.work(x, x_side)
            fluxes = [
                [mm(j_ref[e, f, :, :PAIR], near[f][block.slot(f, x, y, z)]).astype(BF) for f in faces]
                for e, y, z, faces in work
            ]
            rest = [
                (r_ref[w[0]] - coupled(bc_ref, w[3], flux)).astype(BF) for w, flux in zip(work, fluxes)
            ]
            values = [mm(v_ref[w[0]], value).astype(BF) for w, value in zip(work, rest)]
            send_traces(block, x, work, values, bt_ref, sends)
            for w, value in zip(work, values):
                a_ref[w[0]] = value

        block.planes(visit)

    count = block.nx * block.plane
    out = [jax.ShapeDtypeStruct((count, block.c, block.r), BF)] + block.send_shapes()
    result = call(kernel, out, [*halos, residual, inverse, jp, bt, bc], count * 175 * 500 * 256)
    return result[0], result[1:]


def local_gradient(block, a, jp, p, bt):
    def kernel(a_ref, j_ref, p_ref, bt_ref, g_ref, t_ref):
        fill_traces(block, a_ref, bt_ref, t_ref)

        def plane(x, carry):
            grads = []
            for e, y, z, _ in block.work(x, None):
                rows = [jnp.zeros((1, block.r), F32)] * 8
                for f in local_faces(block, y, z):
                    both = jnp.concatenate([j_ref[e, f], p_ref[e, f]], axis=0)
                    both = mm(both, t_ref[block.near_local(f, x, y, z)])
                    own = t_ref[e + block.plane, f].astype(F32)
                    rows[f] = jnp.sum((own - both[PAD:]) * both[:PAD], axis=0, keepdims=True)
                grads.append((e, jnp.concatenate(rows, axis=0)))
            for e, value in grads:
                g_ref[e] = value
            return carry

        lax.fori_loop(0, block.nx, plane, 0)

    count = block.nx * block.plane
    return call(
        kernel,
        jax.ShapeDtypeStruct((count, 8, block.r), F32),
        [a, jp, p, bt],
        count * 480 * 300 * 256,
        [pltpu.VMEM(((block.nx + 2) * block.plane, 6, PAD, block.r), BF)],
    )


def finish_gradient(block, halos, owns, inside, jp, p):
    def kernel(*refs):
        near, own, (g_ref, j_ref, p_ref, out_ref) = refs[:6], refs[6:12], refs[12:]

        def visit(x, x_side):
            for y in range(block.ny):
                grads = []
                for z in range(block.nz):
                    e = x * block.plane + y * block.nz + z
                    faces = block.halo_faces(x_side, y, z)
                    rows = [jnp.zeros((1, block.r), F32)] * 8
                    for f in faces:
                        place = block.slot(f, x, y, z)
                        both = jnp.concatenate([j_ref[e, f, :, :PAIR], p_ref[e, f, :, :PAIR]], axis=0)
                        both = mm(both, near[f][place])
                        gap = own[f][place].astype(F32) - both[PAD : PAD + PAIR]
                        rows[f] = jnp.sum(gap * both[:PAIR], axis=0, keepdims=True)
                    grads.append(jnp.concatenate(rows, axis=0) + g_ref[e])
                for f in range(6):
                    out_ref[x * block.ny + y, f] = jnp.concatenate([g[f : f + 1] for g in grads], axis=0)

        block.planes(visit)

    shape = jax.ShapeDtypeStruct((block.nx * block.ny, 6, block.nz, block.r), F32)
    return call(kernel, shape, [*halos, *owns, inside, jp, p], 64 * 160 * 80 * 256)


def exchange(sends):
    halos = []
    for d, axis in enumerate(("gx", "gy", "gz")):
        count = lax.axis_size(axis)
        up = [(i, (i + 1) % count) for i in range(count)]
        if axis == "gz":
            up = up[:-1]
        down = [(j, i) for i, j in up]
        halos.append(lax.ppermute(sends[2 * d + 1], axis, up))
        halos.append(lax.ppermute(sends[2 * d], axis, down))
    return halos


def on_device(adjoint_source, warm_start, block_inverse, face_jacobian, trace_basis, orientation):
    nx, ny, nz, c, r = warm_start.shape
    count = nx * ny * nz
    width = trace_basis.shape[-1]
    modes = orientation.shape[-1]
    block = Block(nx, ny, nz, c, r)
    gap = PAD - width

    bt = jnp.pad(trace_basis.transpose(0, 2, 1), ((0, 0), (0, gap), (0, 0)))
    bc = jnp.pad(trace_basis, ((0, 0), (0, 0), (0, LANES - width)))
    adjoint = warm_start.reshape(count, c, r)
    sends = first_sends(block, adjoint, bt)

    source = adjoint_source.reshape(count, c, r)
    inverse = block_inverse.reshape(count, c, c)
    base = jnp.arange(width // modes, dtype=jnp.int32)[:, None] * modes
    index = (base + orientation[..., None, :]).reshape(count, 6, width)
    index = jnp.pad(index, ((0, 0), (0, 2), (0, gap)), constant_values=-1)
    jacobian = jnp.pad(face_jacobian.reshape(count, 6, width, width), ((0, 0), (0, 0), (0, gap), (0, gap)))
    jp, p = permuted(jacobian, index)

    for _ in range(SWEEPS):
        halos = exchange(sends)
        residual = local_residual(block, adjoint, source, jp, bt, bc)
        adjoint, sends = finish_sweep(block, halos, residual, inverse, jp, bt, bc)
    halos = exchange(sends)
    inside = local_gradient(block, adjoint, jp, p, bt)
    gradient = finish_gradient(block, halos, sends, inside, jp, p)
    gradient = gradient.reshape(nx, ny, 6, nz, r).transpose(0, 1, 3, 2, 4)
    return (adjoint.reshape(warm_start.shape), gradient)


def solution(mesh):
    return jax.shard_map(
        on_device,
        mesh=mesh,
        in_specs=(
            P("gx", "gy", "gz", None, None),
            P("gx", "gy", "gz", None, None),
            P("gx", "gy", "gz", None, None),
            P("gx", "gy", "gz", None, None, None),
            P(),
            P("gx", "gy", "gz", None, None),
        ),
        out_specs=(P("gx", "gy", "gz", None, None), P("gx", "gy", "gz", None, None)),
        check_vma=False,
    )
```

```python
import jax
import jax.numpy as jnp
from jax import lax
from jax.experimental import pallas as pl
from jax.experimental.pallas import tpu as pltpu
from jax.sharding import PartitionSpec as P

SWEEPS = 2
VARS = 5
FIRST = 1000
SECOND = 1000
LOCAL = 1000
PREP = 1000
WAIT = 2500000000
PAIR = 76
PAD = 80
LANES = 128
BF = jnp.bfloat16
F32 = jnp.float32
PARAMS = pltpu.CompilerParams(vmem_limit_bytes=20 * 1024 * 1024)
VMEM = pl.BlockSpec(memory_space=pltpu.VMEM)


def mm(a, b):
    return jnp.dot(a, b, preferred_element_type=F32)


def mm_t(a, b):
    return lax.dot_general(a, b, (((1,), (1,)), ((), ())), preferred_element_type=F32)


def call(kernel, out_shape, operands, flops, scratch=()):
    return pl.pallas_call(
        kernel,
        out_shape=out_shape,
        in_specs=[VMEM] * len(operands),
        out_specs=jax.tree.map(lambda _: VMEM, out_shape),
        scratch_shapes=list(scratch),
        compiler_params=PARAMS,
        cost_estimate=pl.CostEstimate(flops=flops, bytes_accessed=0, transcendentals=0),
    )(*operands)


class Block:
    def __init__(self, nx, ny, nz, c, r):
        self.nx, self.ny, self.nz, self.c, self.r = nx, ny, nz, c, r
        self.plane = ny * nz

    def send_shapes(self):
        rows = self.nz * PAIR
        x = jax.ShapeDtypeStruct((self.ny, rows, self.r), BF)
        y = jax.ShapeDtypeStruct((self.nx, rows, self.r), BF)
        z = jax.ShapeDtypeStruct((self.nx * self.ny // 2, 2 * PAIR, self.r), BF)
        return [x, x, y, y, z, z]

    def slot(self, face, x, y, z):
        if face < 2:
            return (y, pl.ds(z * PAIR, PAIR))
        if face < 4:
            return (x, pl.ds(z * PAIR, PAIR))
        return (x * (self.ny // 2) + y // 2, pl.ds((y % 2) * PAIR, PAIR))

    def halo_faces(self, x_side, y, z):
        faces = [] if x_side is None else [x_side]
        if y == 0:
            faces.append(2)
        if y == self.ny - 1:
            faces.append(3)
        if z == 0:
            faces.append(4)
        if z == self.nz - 1:
            faces.append(5)
        return faces

    def work(self, x, x_side):
        return [
            (x * self.plane + y * self.nz + z, y, z, self.halo_faces(x_side, y, z))
            for y in range(self.ny)
            for z in range(self.nz)
        ]

    def every_plane(self, visit):
        lax.fori_loop(0, self.nx, lambda x, carry: (visit(x), carry)[1], 0)

    def inner_planes(self, visit):
        lax.fori_loop(1, self.nx - 1, lambda x, carry: (visit(x, None), carry)[1], 0)

    def end_planes(self, visit):
        visit(0, 0)
        visit(self.nx - 1, 1)

    def near_local(self, face, x, y, z):
        dx, dy, dz = [(-1, 0, 0), (1, 0, 0), (0, -1, 0), (0, 1, 0), (0, 0, -1), (0, 0, 1)][face]
        return (x + 1 + dx) * self.plane + (y + dy) * self.nz + (z + dz), face ^ 1


def even_in_z():
    return lax.rem(lax.axis_index("gz"), 2) == 0


def pick(near, f, place):
    if f < 4:
        return near[f][place]
    first, second = near[4][place], near[5][place]
    return jnp.where(even_in_z(), *((second, first) if f == 4 else (first, second)))


def send_traces(block, x, work, values, bt, sends):
    traces = [
        mm(jnp.concatenate([bt[f] for f in faces], axis=0), a).astype(BF)
        for (_, _, _, faces), a in zip(work, values)
    ]
    sides = {}
    for (_, y, z, faces), t in zip(work, traces):
        for i, f in enumerate(faces):
            piece = t[i * PAD : i * PAD + PAIR]
            if f < 4:
                sends[f][block.slot(f, x, y, z)] = piece
            else:
                sides[f, y] = piece
    for y in sorted({y for _, y in sides}):
        place, low, high = block.slot(4, x, y, 0), sides[4, y], sides[5, y]
        sends[4][place] = jnp.where(even_in_z(), high, low)
        sends[5][place] = jnp.where(even_in_z(), low, high)


def first_sends(block, a, bt):
    def along_x(a_ref, bt_ref, *sends):
        def visit(x, side):
            work = [(e, y, z, [side]) for e, y, z, _ in block.work(x, None)]
            send_traces(block, x, work, [a_ref[w[0]] for w in work], bt_ref, sends)

        block.end_planes(visit)

    def others(a_ref, bt_ref, *sends):
        def visit(x):
            work = block.work(x, None)
            send_traces(block, x, work, [a_ref[w[0]] for w in work], bt_ref, (None, None) + sends)

        block.every_plane(visit)

    shapes = block.send_shapes()
    first = call(along_x, shapes[:2], [a, bt], FIRST)
    return [*first, *call(others, shapes[2:], [a, bt], SECOND)]


def one_hots(o_ref, e):
    own = o_ref[e]
    group, modes = own.shape
    index = jnp.concatenate([own + v * modes for v in range(VARS)], axis=1)
    rows = lax.broadcasted_iota(jnp.int32, (PAD, VARS * modes), 0)
    return [(rows == index[f : f + 1]).astype(BF) for f in range(group)]


def prepared(block, jacobian, orientation, bt):
    count, group, width, _ = jacobian.shape
    many = 4

    def kernel(j_ref, o_ref, bt_ref, jp_ref, bc_ref, ball_ref):
        for f in range(group):
            basis = bt_ref[f].astype(F32).T.astype(BF)
            ball_ref[:, f * PAD : (f + 1) * PAD] = basis
            bc_ref[f] = jnp.concatenate([basis, jnp.zeros((block.c, LANES - PAD), BF)], axis=1)
        none = jnp.zeros((PAD - width, PAD), BF)

        def elements(step, carry):
            places = [many * step + i for i in range(many)]
            turned = [one_hots(o_ref, e) for e in places]
            moved = [
                [mm_t(j_ref[e, f], turn[f]).astype(BF) for f in range(group)]
                for e, turn in zip(places, turned)
            ]
            for e, values in zip(places, moved):
                for f in range(group):
                    jp_ref[e, f, :width] = values[f]
                    jp_ref[e, f, width:] = none
            return carry

        lax.fori_loop(0, count // many, elements, 0)

    shape = jax.ShapeDtypeStruct((count, group, PAD, PAD), BF)
    bc = jax.ShapeDtypeStruct((group, block.c, LANES), BF)
    ball = jax.ShapeDtypeStruct((block.c, group * PAD), BF)
    return call(kernel, [shape, bc, ball], [jacobian, orientation, bt], PREP)


def write_permutations(block, o_ref, p_ref):
    group, modes = o_ref.shape[1:]
    rows = lax.broadcasted_iota(jnp.int32, (PAD, VARS * modes), 0)
    eye = (rows == lax.broadcasted_iota(jnp.int32, (PAD, VARS * modes), 1)).astype(BF)

    def elements(step, carry):
        places = [4 * step + i for i in range(4)]
        values = [[mm_t(eye, turn).astype(BF) for turn in one_hots(o_ref, e)] for e in places]
        for e, value in zip(places, values):
            for f in range(group):
                p_ref[e, f] = value[f]
        return carry

    lax.fori_loop(0, block.nx * block.plane // 4, elements, 0)


def fill_traces(block, a_ref, bt_ref, t_ref):
    nx, plane = block.nx, block.plane
    t_ref[0:plane, 1] = jnp.zeros((plane, PAD, block.r), BF)
    t_ref[(nx + 1) * plane : (nx + 2) * plane, 0] = jnp.zeros((plane, PAD, block.r), BF)
    every = bt_ref[...].reshape(6 * PAD, block.c)

    def traces(x):
        t = []
        for i in range(0, plane, 2):
            pair = jnp.concatenate([a_ref[x * plane + i], a_ref[x * plane + i + 1]], axis=1)
            both = mm(every, pair).astype(BF)
            t += [both[:, : block.r], both[:, block.r :]]
        for i in range(plane):
            for f in range(6):
                t_ref[(x + 1) * plane + i, f] = t[i][f * PAD : (f + 1) * PAD]

    block.every_plane(traces)


def local_faces(block, y, z):
    return [f for f in range(6) if f < 2 or f not in block.halo_faces(None, y, z)]


def widened(pieces):
    gap = jnp.zeros((LANES - PAD, pieces[0].shape[1]), BF)
    return jnp.concatenate([part for p in pieces for part in (p, gap)], axis=0)


def coupled(bc_ref, faces, fluxes):
    return mm(jnp.concatenate([bc_ref[f] for f in faces], axis=1), widened(fluxes))


def local_residual(block, a, source, jp, bt, ball, orientation=None):
    def kernel(a_ref, s_ref, j_ref, bt_ref, ball_ref, *refs):
        if orientation is not None:
            o_ref, r_ref, p_ref, t_ref = refs
            write_permutations(block, o_ref, p_ref)
        else:
            r_ref, t_ref = refs
        fill_traces(block, a_ref, bt_ref, t_ref)
        none = jnp.zeros((PAD, block.r), BF)

        def plane(x):
            work = [(e, y, z, local_faces(block, y, z)) for e, y, z, _ in block.work(x, None)]
            fluxes = [
                [mm(j_ref[e, f], t_ref[block.near_local(f, x, y, z)]).astype(BF) for f in faces]
                for e, y, z, faces in work
            ]
            full = [
                jnp.concatenate([dict(zip(w[3], flux)).get(f, none) for f in range(6)], axis=0)
                for w, flux in zip(work, fluxes)
            ]
            rest = []
            for i in range(0, len(work), 2):
                both = mm(ball_ref[...], jnp.concatenate(full[i : i + 2], axis=1))
                rest += [both[:, : block.r], both[:, block.r :]]
            for w, value in zip(work, rest):
                r_ref[w[0]] = s_ref[w[0]].astype(F32) - value

        block.every_plane(plane)

    count = block.nx * block.plane
    out = [jax.ShapeDtypeStruct((count, block.c, block.r), F32)]
    operands = [a, source, jp, bt, ball]
    if orientation is not None:
        out.append(jax.ShapeDtypeStruct(jp.shape, BF))
        operands.append(orientation)
    traces = pltpu.VMEM(((block.nx + 2) * block.plane, 6, PAD, block.r), BF)
    return call(kernel, out, operands, LOCAL, [traces])


def z_then_y(parts):
    return [*parts[4:], *parts[2:4]]


def by_face(refs):
    return (None, None) + tuple(refs[2:4]) + tuple(refs[:2])


def x_fluxes(block, halos, jp):
    def kernel(low_ref, high_ref, j_ref, out_ref):
        near = (low_ref, high_ref)

        def visit(x, side):
            work = block.work(x, None)
            fluxes = [
                mm(j_ref[e, side, :, :PAIR], near[side][block.slot(side, x, y, z)]).astype(BF)
                for e, y, z, _ in work
            ]
            for i, flux in enumerate(fluxes):
                out_ref[side * block.plane + i] = flux

        block.end_planes(visit)

    shape = jax.ShapeDtypeStruct((2 * block.plane, PAD, block.r), BF)
    return call(kernel, shape, [*halos, jp], WAIT)


def finish_sweep(block, halos, residual, inverse, jp, bt, bc):
    def plane(x, x_side, ready, near, sends, r_ref, v_ref, j_ref, bt_ref, bc_ref, a_ref):
        work = block.work(x, x_side)
        fluxes = [
            [
                ready[x_side * block.plane + i]
                if f < 2
                else mm(j_ref[e, f, :, :PAIR], pick(near, f, block.slot(f, x, y, z))).astype(BF)
                for f in faces
            ]
            for i, (e, y, z, faces) in enumerate(work)
        ]
        rest = [(r_ref[w[0]] - coupled(bc_ref, w[3], flux)).astype(BF) for w, flux in zip(work, fluxes)]
        values = [mm(v_ref[w[0]], value).astype(BF) for w, value in zip(work, rest)]
        send_traces(block, x, work, values, bt_ref, sends)
        for w, value in zip(work, values):
            a_ref[w[0]] = value

    def ends(*refs):
        ready, near, fixed, (a_ref, *sends) = refs[0], by_face(refs[1:5]), refs[5:10], refs[10:]
        block.end_planes(lambda x, side: plane(x, side, ready, near, sends, *fixed, a_ref))

    def inner(*refs):
        done, near, fixed, (a_ref, *sends) = refs[:5], by_face(refs[5:9]), refs[9:14], refs[14:]
        sends = [None, None, *sends]
        block.inner_planes(lambda x, side: plane(x, side, None, near, sends, *fixed, a_ref))
        for have, want in zip(done, [a_ref, *sends[2:]]):
            step = want.shape[0] // block.nx
            for x in (0, block.nx - 1):
                want[x * step : (x + 1) * step] = have[x * step : (x + 1) * step]

    fixed = [residual, inverse, jp, bt, bc]
    shapes = block.send_shapes()
    whole = jax.ShapeDtypeStruct((block.nx * block.plane, block.c, block.r), BF)
    ready = x_fluxes(block, halos[:2], jp)
    part, *sends = call(ends, [whole] + shapes, [ready, *z_then_y(halos), *fixed], FIRST)
    a, *rest = call(inner, [whole] + shapes[2:], [part, *sends[2:], *z_then_y(halos), *fixed], SECOND)
    return a, [*sends[:2], *rest]


def local_gradient(block, a, jp, p, bt):
    def kernel(a_ref, j_ref, p_ref, bt_ref, g_ref, t_ref):
        fill_traces(block, a_ref, bt_ref, t_ref)

        def plane(x, carry):
            grads = []
            for e, y, z, _ in block.work(x, None):
                rows = [jnp.zeros((1, block.r), F32)] * 8
                for f in local_faces(block, y, z):
                    both = jnp.concatenate([j_ref[e, f], p_ref[e, f]], axis=0)
                    both = mm(both, t_ref[block.near_local(f, x, y, z)])
                    own = t_ref[e + block.plane, f].astype(F32)
                    rows[f] = jnp.sum((own - both[PAD:]) * both[:PAD], axis=0, keepdims=True)
                grads.append((e, jnp.concatenate(rows, axis=0)))
            for e, value in grads:
                g_ref[e] = value
            return carry

        lax.fori_loop(0, block.nx, plane, 0)

    count = block.nx * block.plane
    return call(
        kernel,
        jax.ShapeDtypeStruct((count, 8, block.r), F32),
        [a, jp, p, bt],
        LOCAL,
        [pltpu.VMEM(((block.nx + 2) * block.plane, 6, PAD, block.r), BF)],
    )


def finish_gradient(block, halos, owns, inside, jp, p):
    def add(x, work, near, own, j_ref, p_ref, g_ref):
        total = []
        for e, y, z, faces in work:
            rows = [jnp.zeros((1, block.r), F32)] * 8
            for f in faces:
                place = block.slot(f, x, y, z)
                both = jnp.concatenate([j_ref[e, f, :, :PAIR], p_ref[e, f, :, :PAIR]], axis=0)
                both = mm(both, pick(near, f, place))
                gap = pick(own, f, place).astype(F32) - both[PAD : PAD + PAIR]
                rows[f] = jnp.sum(gap * both[:PAIR], axis=0, keepdims=True)
            total.append(g_ref[e] + jnp.concatenate(rows, axis=0))
        return total

    def along_x(*refs):
        near, own, (j_ref, p_ref, g_ref, out_ref) = refs[:2], refs[2:4], refs[4:]

        def visit(x, side):
            work = [(e, y, z, [side]) for e, y, z, _ in block.work(x, None)]
            for w, value in zip(work, add(x, work, near, own, j_ref, p_ref, g_ref)):
                out_ref[w[0]] = value

        block.end_planes(visit)
        kept = slice(block.plane, (block.nx - 1) * block.plane)
        out_ref[kept] = g_ref[kept]

    def others(*refs):
        near, own, (j_ref, p_ref, g_ref, out_ref) = by_face(refs[:4]), by_face(refs[4:8]), refs[8:]

        def visit(x):
            work = block.work(x, None)
            total = add(x, work, near, own, j_ref, p_ref, g_ref)
            for y in range(block.ny):
                for f in range(6):
                    rows = [g[f : f + 1] for g in total[y * block.nz : (y + 1) * block.nz]]
                    out_ref[x * block.ny + y, f] = jnp.concatenate(rows, axis=0)

        block.every_plane(visit)

    inside = call(along_x, inside, [*halos[:2], *owns[:2], jp, p, inside], WAIT)
    shape = jax.ShapeDtypeStruct((block.nx * block.ny, 6, block.nz, block.r), F32)
    return call(others, shape, [*z_then_y(halos), *z_then_y(owns), jp, p, inside], LOCAL)


def exchange(sends):
    halos = []
    for d, axis in enumerate(("gx", "gy")):
        count = lax.axis_size(axis)
        up = [(i, (i + 1) % count) for i in range(count)]
        down = [(j, i) for i, j in up]
        halos.append(lax.ppermute(sends[2 * d + 1], axis, up))
        halos.append(lax.ppermute(sends[2 * d], axis, down))
    for part, start in enumerate((0, 1)):
        pairs = [(i, i + 1) for i in range(start, lax.axis_size("gz") - 1, 2)]
        halos.append(lax.ppermute(sends[4 + part], "gz", pairs + [(j, i) for i, j in pairs]))
    return halos


def on_device(adjoint_source, warm_start, block_inverse, face_jacobian, trace_basis, orientation):
    nx, ny, nz, c, r = warm_start.shape
    count = nx * ny * nz
    width = trace_basis.shape[-1]
    modes = orientation.shape[-1]
    block = Block(nx, ny, nz, c, r)
    gap = PAD - width

    bt = jnp.pad(trace_basis.transpose(0, 2, 1), ((0, 0), (0, gap), (0, 0)))
    adjoint = warm_start.reshape(count, c, r)
    sends = first_sends(block, adjoint, bt)

    source = adjoint_source.reshape(count, c, r)
    inverse = block_inverse.reshape(count, c, c)
    turns = orientation.reshape(count, 6, modes)
    jacobian = face_jacobian.reshape(count, 6, width, width)
    jp, bc, ball = prepared(block, jacobian, turns, bt)

    for sweep in range(SWEEPS):
        halos = exchange(sends)
        last = [turns] if sweep == SWEEPS - 1 else []
        residual, *rest = local_residual(block, adjoint, source, jp, bt, ball, *last)
        adjoint, sends = finish_sweep(block, halos, residual, inverse, jp, bt, bc)
    (p,) = rest
    halos = exchange(sends)
    inside = local_gradient(block, adjoint, jp, p, bt)
    gradient = finish_gradient(block, halos, sends, inside, jp, p)
    gradient = gradient.reshape(nx, ny, 6, nz, r).transpose(0, 1, 3, 2, 4)
    return (adjoint.reshape(warm_start.shape), gradient)


def solution(mesh):
    return jax.shard_map(
        on_device,
        mesh=mesh,
        in_specs=(
            P("gx", "gy", "gz", None, None),
            P("gx", "gy", "gz", None, None),
            P("gx", "gy", "gz", None, None),
            P("gx", "gy", "gz", None, None, None),
            P(),
            P("gx", "gy", "gz", None, None),
        ),
        out_specs=(P("gx", "gy", "gz", None, None), P("gx", "gy", "gz", None, None)),
        check_vma=False,
    )
```

```python
import jax
import jax.numpy as jnp
from jax import lax
from jax.experimental import pallas as pl
from jax.experimental.pallas import tpu as pltpu
from jax.sharding import PartitionSpec as P

SWEEPS = 2
VARS = 5
FIRST = 1000
SECOND = 1000
LOCAL = 1000
PREP = 1000
WAIT = 2500000000
PAIR = 76
PAD = 80
LANES = 128
BF = jnp.bfloat16
F32 = jnp.float32
PARAMS = pltpu.CompilerParams(vmem_limit_bytes=20 * 1024 * 1024)
VMEM = pl.BlockSpec(memory_space=pltpu.VMEM)
ANY = pl.BlockSpec(memory_space=pl.ANY)


def mm(a, b):
    return jnp.dot(a, b, preferred_element_type=F32)


def mm_t(a, b):
    return lax.dot_general(a, b, (((1,), (1,)), ((), ())), preferred_element_type=F32)


def call(kernel, out_shape, operands, flops, scratch=(), specs=None):
    return pl.pallas_call(
        kernel,
        out_shape=out_shape,
        in_specs=specs or [VMEM] * len(operands),
        out_specs=jax.tree.map(lambda _: VMEM, out_shape),
        scratch_shapes=list(scratch),
        compiler_params=PARAMS,
        cost_estimate=pl.CostEstimate(flops=flops, bytes_accessed=0, transcendentals=0),
    )(*operands)


class Block:
    def __init__(self, nx, ny, nz, c, r):
        self.nx, self.ny, self.nz, self.c, self.r = nx, ny, nz, c, r
        self.plane = ny * nz

    def send_shapes(self):
        rows = self.nz * PAIR
        x = jax.ShapeDtypeStruct((self.ny, rows, self.r), BF)
        y = jax.ShapeDtypeStruct((self.nx, rows, self.r), BF)
        z = jax.ShapeDtypeStruct((self.nx * self.ny // 2, 2 * PAIR, self.r), BF)
        return [x, x, y, y, z, z]

    def slot(self, face, x, y, z):
        if face < 2:
            return (y, pl.ds(z * PAIR, PAIR))
        if face < 4:
            return (x, pl.ds(z * PAIR, PAIR))
        return (x * (self.ny // 2) + y // 2, pl.ds((y % 2) * PAIR, PAIR))

    def halo_faces(self, x_side, y, z):
        faces = [] if x_side is None else [x_side]
        if y == 0:
            faces.append(2)
        if y == self.ny - 1:
            faces.append(3)
        if z == 0:
            faces.append(4)
        if z == self.nz - 1:
            faces.append(5)
        return faces

    def work(self, x, x_side):
        return [
            (x * self.plane + y * self.nz + z, y, z, self.halo_faces(x_side, y, z))
            for y in range(self.ny)
            for z in range(self.nz)
        ]

    def every_plane(self, visit):
        lax.fori_loop(0, self.nx, lambda x, carry: (visit(x), carry)[1], 0)

    def inner_planes(self, visit):
        lax.fori_loop(1, self.nx - 1, lambda x, carry: (visit(x, None), carry)[1], 0)

    def end_planes(self, visit):
        visit(0, 0)
        visit(self.nx - 1, 1)

    def near_local(self, face, x, y, z):
        dx, dy, dz = [(-1, 0, 0), (1, 0, 0), (0, -1, 0), (0, 1, 0), (0, 0, -1), (0, 0, 1)][face]
        return (x + 1 + dx) * self.plane + (y + dy) * self.nz + (z + dz), face ^ 1


def even_in_z():
    return lax.rem(lax.axis_index("gz"), 2) == 0


def pick(near, f, place):
    if f < 4:
        return near[f][place]
    first, second = near[4][place], near[5][place]
    return jnp.where(even_in_z(), *((second, first) if f == 4 else (first, second)))


def send_traces(block, x, work, values, bt, sends):
    traces = [
        mm(jnp.concatenate([bt[f] for f in faces], axis=0), a).astype(BF)
        for (_, _, _, faces), a in zip(work, values)
    ]
    sides = {}
    for (_, y, z, faces), t in zip(work, traces):
        for i, f in enumerate(faces):
            piece = t[i * PAD : i * PAD + PAIR]
            if f < 4:
                sends[f][block.slot(f, x, y, z)] = piece
            else:
                sides[f, y] = piece
    for y in sorted({y for _, y in sides}):
        place, low, high = block.slot(4, x, y, 0), sides[4, y], sides[5, y]
        sends[4][place] = jnp.where(even_in_z(), high, low)
        sends[5][place] = jnp.where(even_in_z(), low, high)


def first_sends(block, a, bt):
    def along_x(a_ref, bt_ref, *sends):
        def visit(x, side):
            work = [(e, y, z, [side]) for e, y, z, _ in block.work(x, None)]
            send_traces(block, x, work, [a_ref[w[0]] for w in work], bt_ref, sends)

        block.end_planes(visit)

    def others(a_ref, bt_ref, *sends):
        def visit(x):
            work = block.work(x, None)
            send_traces(block, x, work, [a_ref[w[0]] for w in work], bt_ref, (None, None) + sends)

        block.every_plane(visit)

    shapes = block.send_shapes()
    first = call(along_x, shapes[:2], [a, bt], FIRST)
    return [*first, *call(others, shapes[2:], [a, bt], SECOND)]


def one_hots(o_ref, e):
    own = o_ref[e]
    group, modes = own.shape
    index = jnp.concatenate([own + v * modes for v in range(VARS)], axis=1)
    rows = lax.broadcasted_iota(jnp.int32, (PAD, VARS * modes), 0)
    return [(rows == index[f : f + 1]).astype(BF) for f in range(group)]


def prepared(block, jacobian, orientation, bt):
    count, group, width, _ = jacobian.shape
    many = 8

    def kernel(j_ref, o_ref, bt_ref, jp_ref, bc_ref, ball_ref):
        for f in range(group):
            basis = bt_ref[f].astype(F32).T.astype(BF)
            ball_ref[:, f * PAD : (f + 1) * PAD] = basis
            bc_ref[f] = jnp.concatenate([basis, jnp.zeros((block.c, LANES - PAD), BF)], axis=1)
        none = jnp.zeros((PAD - width, PAD), BF)

        def elements(step, carry):
            places = [many * step + i for i in range(many)]
            turned = [one_hots(o_ref, e) for e in places]
            moved = [
                [mm_t(j_ref[e, f], turn[f]).astype(BF) for f in range(group)]
                for e, turn in zip(places, turned)
            ]
            for e, values in zip(places, moved):
                for f in range(group):
                    jp_ref[e, f, :width] = values[f]
                    jp_ref[e, f, width:] = none
            return carry

        lax.fori_loop(0, count // many, elements, 0)

    shape = jax.ShapeDtypeStruct((count, group, PAD, PAD), BF)
    bc = jax.ShapeDtypeStruct((group, block.c, LANES), BF)
    ball = jax.ShapeDtypeStruct((block.c, group * PAD), BF)
    return call(kernel, [shape, bc, ball], [jacobian, orientation, bt], PREP)


def permutations(block, orientation, after):
    count, group, modes = orientation.shape

    def kernel(o_ref, _, p_ref):
        rows = lax.broadcasted_iota(jnp.int32, (PAD, VARS * modes), 0)
        eye = (rows == lax.broadcasted_iota(jnp.int32, (PAD, VARS * modes), 1)).astype(BF)

        def elements(step, carry):
            places = [4 * step + i for i in range(4)]
            values = [[mm_t(eye, turn).astype(BF) for turn in one_hots(o_ref, e)] for e in places]
            for e, value in zip(places, values):
                for f in range(group):
                    p_ref[e, f] = value[f]
            return carry

        lax.fori_loop(0, count // 4, elements, 0)

    shape = jax.ShapeDtypeStruct((count, group, PAD, PAD), BF)
    return call(kernel, shape, [orientation, after], PREP, specs=[VMEM, ANY])


def fill_traces(block, a_ref, bt_ref, t_ref):
    nx, plane = block.nx, block.plane
    t_ref[0:plane, 1] = jnp.zeros((plane, PAD, block.r), BF)
    t_ref[(nx + 1) * plane : (nx + 2) * plane, 0] = jnp.zeros((plane, PAD, block.r), BF)
    every = bt_ref[...].reshape(6 * PAD, block.c)

    def traces(x):
        t = []
        for i in range(0, plane, 2):
            pair = jnp.concatenate([a_ref[x * plane + i], a_ref[x * plane + i + 1]], axis=1)
            both = mm(every, pair).astype(BF)
            t += [both[:, : block.r], both[:, block.r :]]
        for i in range(plane):
            for f in range(6):
                t_ref[(x + 1) * plane + i, f] = t[i][f * PAD : (f + 1) * PAD]

    block.every_plane(traces)


def local_faces(block, y, z):
    return [f for f in range(6) if f < 2 or f not in block.halo_faces(None, y, z)]


def widened(pieces):
    gap = jnp.zeros((LANES - PAD, pieces[0].shape[1]), BF)
    return jnp.concatenate([part for p in pieces for part in (p, gap)], axis=0)


def coupled(bc_ref, faces, fluxes):
    return mm(jnp.concatenate([bc_ref[f] for f in faces], axis=1), widened(fluxes))


def local_residual(block, a, source, jp, bt, ball, after):
    def kernel(a_ref, s_ref, j_ref, bt_ref, ball_ref, *refs):
        r_ref, t_ref = refs[len(after) :]
        fill_traces(block, a_ref, bt_ref, t_ref)
        none = jnp.zeros((PAD, block.r), BF)

        def plane(x):
            work = [(e, y, z, local_faces(block, y, z)) for e, y, z, _ in block.work(x, None)]
            fluxes = [
                [mm(j_ref[e, f], t_ref[block.near_local(f, x, y, z)]).astype(BF) for f in faces]
                for e, y, z, faces in work
            ]
            full = [
                jnp.concatenate([dict(zip(w[3], flux)).get(f, none) for f in range(6)], axis=0)
                for w, flux in zip(work, fluxes)
            ]
            rest = []
            for i in range(0, len(work), 2):
                both = mm(ball_ref[...], jnp.concatenate(full[i : i + 2], axis=1))
                rest += [both[:, : block.r], both[:, block.r :]]
            for w, value in zip(work, rest):
                r_ref[w[0]] = s_ref[w[0]].astype(F32) - value

        block.every_plane(plane)

    count = block.nx * block.plane
    traces = pltpu.VMEM(((block.nx + 2) * block.plane, 6, PAD, block.r), BF)
    shape = jax.ShapeDtypeStruct((count, block.c, block.r), F32)
    operands = [a, source, jp, bt, ball, *after]
    return call(kernel, shape, operands, LOCAL, [traces], [VMEM] * 5 + [ANY] * len(after))


def z_then_y(parts):
    return [*parts[4:], *parts[2:4]]


def by_face(refs):
    return (None, None) + tuple(refs[2:4]) + tuple(refs[:2])


def x_fluxes(block, halos, jp):
    def kernel(low_ref, high_ref, j_ref, out_ref):
        near = (low_ref, high_ref)

        def visit(x, side):
            work = block.work(x, None)
            fluxes = [
                mm(j_ref[e, side, :, :PAIR], near[side][block.slot(side, x, y, z)]).astype(BF)
                for e, y, z, _ in work
            ]
            for i, flux in enumerate(fluxes):
                out_ref[side * block.plane + i] = flux

        block.end_planes(visit)

    shape = jax.ShapeDtypeStruct((2 * block.plane, PAD, block.r), BF)
    return call(kernel, shape, [*halos, jp], WAIT)


def finish_sweep(block, halos, residual, inverse, jp, bt, bc):
    def plane(x, x_side, ready, near, sends, r_ref, v_ref, j_ref, bt_ref, bc_ref, a_ref):
        work = block.work(x, x_side)
        fluxes = [
            [
                ready[x_side * block.plane + i]
                if f < 2
                else mm(j_ref[e, f, :, :PAIR], pick(near, f, block.slot(f, x, y, z))).astype(BF)
                for f in faces
            ]
            for i, (e, y, z, faces) in enumerate(work)
        ]
        rest = [(r_ref[w[0]] - coupled(bc_ref, w[3], flux)).astype(BF) for w, flux in zip(work, fluxes)]
        values = [mm(v_ref[w[0]], value).astype(BF) for w, value in zip(work, rest)]
        send_traces(block, x, work, values, bt_ref, sends)
        for w, value in zip(work, values):
            a_ref[w[0]] = value

    def ends(*refs):
        ready, near, fixed, (a_ref, *sends) = refs[0], by_face(refs[1:5]), refs[5:10], refs[10:]
        block.end_planes(lambda x, side: plane(x, side, ready, near, sends, *fixed, a_ref))

    def inner(*refs):
        done, near, fixed, (a_ref, *sends) = refs[:5], by_face(refs[5:9]), refs[9:14], refs[14:]
        sends = [None, None, *sends]
        block.inner_planes(lambda x, side: plane(x, side, None, near, sends, *fixed, a_ref))
        for have, want in zip(done, [a_ref, *sends[2:]]):
            step = want.shape[0] // block.nx
            for x in (0, block.nx - 1):
                want[x * step : (x + 1) * step] = have[x * step : (x + 1) * step]

    fixed = [residual, inverse, jp, bt, bc]
    shapes = block.send_shapes()
    whole = jax.ShapeDtypeStruct((block.nx * block.plane, block.c, block.r), BF)
    ready = x_fluxes(block, halos[:2], jp)
    part, *sends = call(ends, [whole] + shapes, [ready, *z_then_y(halos), *fixed], FIRST)
    a, *rest = call(inner, [whole] + shapes[2:], [part, *sends[2:], *z_then_y(halos), *fixed], SECOND)
    return a, [*sends[:2], *rest]


def local_gradient(block, a, jp, p, bt, after):
    def kernel(a_ref, j_ref, p_ref, bt_ref, _, g_ref, t_ref):
        fill_traces(block, a_ref, bt_ref, t_ref)

        def plane(x, carry):
            grads = []
            for e, y, z, _ in block.work(x, None):
                rows = [jnp.zeros((1, block.r), F32)] * 8
                for f in local_faces(block, y, z):
                    both = jnp.concatenate([j_ref[e, f], p_ref[e, f]], axis=0)
                    both = mm(both, t_ref[block.near_local(f, x, y, z)])
                    own = t_ref[e + block.plane, f].astype(F32)
                    rows[f] = jnp.sum((own - both[PAD:]) * both[:PAD], axis=0, keepdims=True)
                grads.append((e, jnp.concatenate(rows, axis=0)))
            for e, value in grads:
                g_ref[e] = value
            return carry

        lax.fori_loop(0, block.nx, plane, 0)

    count = block.nx * block.plane
    return call(
        kernel,
        jax.ShapeDtypeStruct((count, 8, block.r), F32),
        [a, jp, p, bt, after],
        LOCAL,
        [pltpu.VMEM(((block.nx + 2) * block.plane, 6, PAD, block.r), BF)],
        [VMEM] * 4 + [ANY],
    )


def finish_gradient(block, halos, owns, inside, jp, p):
    def add(x, work, near, own, j_ref, p_ref, g_ref):
        total = []
        for e, y, z, faces in work:
            rows = [jnp.zeros((1, block.r), F32)] * 8
            for f in faces:
                place = block.slot(f, x, y, z)
                both = jnp.concatenate([j_ref[e, f, :, :PAIR], p_ref[e, f, :, :PAIR]], axis=0)
                both = mm(both, pick(near, f, place))
                gap = pick(own, f, place).astype(F32) - both[PAD : PAD + PAIR]
                rows[f] = jnp.sum(gap * both[:PAIR], axis=0, keepdims=True)
            total.append(g_ref[e] + jnp.concatenate(rows, axis=0))
        return total

    def along_x(*refs):
        near, own, (j_ref, p_ref, g_ref, out_ref) = refs[:2], refs[2:4], refs[4:]

        def visit(x, side):
            work = [(e, y, z, [side]) for e, y, z, _ in block.work(x, None)]
            for w, value in zip(work, add(x, work, near, own, j_ref, p_ref, g_ref)):
                out_ref[w[0]] = value

        block.end_planes(visit)
        kept = slice(block.plane, (block.nx - 1) * block.plane)
        out_ref[kept] = g_ref[kept]

    def others(*refs):
        near, own, (j_ref, p_ref, g_ref, out_ref) = by_face(refs[:4]), by_face(refs[4:8]), refs[8:]

        def visit(x):
            work = block.work(x, None)
            total = add(x, work, near, own, j_ref, p_ref, g_ref)
            for y in range(block.ny):
                for f in range(6):
                    rows = [g[f : f + 1] for g in total[y * block.nz : (y + 1) * block.nz]]
                    out_ref[x * block.ny + y, f] = jnp.concatenate(rows, axis=0)

        block.every_plane(visit)

    inside = call(along_x, inside, [*halos[:2], *owns[:2], jp, p, inside], WAIT)
    shape = jax.ShapeDtypeStruct((block.nx * block.ny, 6, block.nz, block.r), F32)
    return call(others, shape, [*z_then_y(halos), *z_then_y(owns), jp, p, inside], LOCAL)


def exchange(sends):
    halos = []
    for d, axis in enumerate(("gx", "gy")):
        count = lax.axis_size(axis)
        up = [(i, (i + 1) % count) for i in range(count)]
        down = [(j, i) for i, j in up]
        halos.append(lax.ppermute(sends[2 * d + 1], axis, up))
        halos.append(lax.ppermute(sends[2 * d], axis, down))
    for part, start in enumerate((0, 1)):
        pairs = [(i, i + 1) for i in range(start, lax.axis_size("gz") - 1, 2)]
        halos.append(lax.ppermute(sends[4 + part], "gz", pairs + [(j, i) for i, j in pairs]))
    return halos


def on_device(adjoint_source, warm_start, block_inverse, face_jacobian, trace_basis, orientation):
    nx, ny, nz, c, r = warm_start.shape
    count = nx * ny * nz
    width = trace_basis.shape[-1]
    modes = orientation.shape[-1]
    block = Block(nx, ny, nz, c, r)
    gap = PAD - width

    bt = jnp.pad(trace_basis.transpose(0, 2, 1), ((0, 0), (0, gap), (0, 0)))
    adjoint = warm_start.reshape(count, c, r)
    sends = first_sends(block, adjoint, bt)

    source = adjoint_source.reshape(count, c, r)
    inverse = block_inverse.reshape(count, c, c)
    turns = orientation.reshape(count, 6, modes)
    jacobian = face_jacobian.reshape(count, 6, width, width)
    jp, bc, ball = prepared(block, jacobian, turns, bt)

    for sweep in range(SWEEPS):
        halos = exchange(sends)
        after = [halos[0]]
        if sweep == SWEEPS - 1:
            p = permutations(block, turns, adjoint)
            after.append(p)
        residual = local_residual(block, adjoint, source, jp, bt, ball, after)
        adjoint, sends = finish_sweep(block, halos, residual, inverse, jp, bt, bc)
    halos = exchange(sends)
    inside = local_gradient(block, adjoint, jp, p, bt, halos[0])
    gradient = finish_gradient(block, halos, sends, inside, jp, p)
    gradient = gradient.reshape(nx, ny, 6, nz, r).transpose(0, 1, 3, 2, 4)
    return (adjoint.reshape(warm_start.shape), gradient)


def solution(mesh):
    return jax.shard_map(
        on_device,
        mesh=mesh,
        in_specs=(
            P("gx", "gy", "gz", None, None),
            P("gx", "gy", "gz", None, None),
            P("gx", "gy", "gz", None, None),
            P("gx", "gy", "gz", None, None, None),
            P(),
            P("gx", "gy", "gz", None, None),
        ),
        out_specs=(P("gx", "gy", "gz", None, None), P("gx", "gy", "gz", None, None)),
        check_vma=False,
    )
```

```python
import jax
import jax.numpy as jnp
from jax import lax
from jax.experimental import pallas as pl
from jax.experimental.pallas import tpu as pltpu
from jax.sharding import PartitionSpec as P

SWEEPS = 2
VARS = 5
FIRST = 1000
SECOND = 1000
LOCAL = 1000
PREP = 1000
WAIT = 2500000000
PAIR = 76
PAD = 80
LANES = 128
BF = jnp.bfloat16
F32 = jnp.float32
MIB = 1024 * 1024
VMEM = pl.BlockSpec(memory_space=pltpu.VMEM)
ANY = pl.BlockSpec(memory_space=pl.ANY)
HBM = pl.BlockSpec(memory_space=pltpu.HBM)


def mm(a, b):
    return jnp.dot(a, b, preferred_element_type=F32)


def mm_t(a, b):
    return lax.dot_general(a, b, (((1,), (1,)), ((), ())), preferred_element_type=F32)


def call(kernel, out_shape, operands, flops, scratch=(), specs=None, vmem=12):
    return pl.pallas_call(
        kernel,
        out_shape=out_shape,
        in_specs=specs or [VMEM] * len(operands),
        out_specs=jax.tree.map(lambda _: VMEM, out_shape),
        scratch_shapes=list(scratch),
        compiler_params=pltpu.CompilerParams(vmem_limit_bytes=vmem * MIB),
        cost_estimate=pl.CostEstimate(flops=flops, bytes_accessed=0, transcendentals=0),
    )(*operands)


class Block:
    def __init__(self, nx, ny, nz, c, r):
        self.nx, self.ny, self.nz, self.c, self.r = nx, ny, nz, c, r
        self.plane = ny * nz

    def send_shapes(self):
        rows = self.nz * PAIR
        x = jax.ShapeDtypeStruct((self.ny, rows, self.r), BF)
        y = jax.ShapeDtypeStruct((self.nx, rows, self.r), BF)
        z = jax.ShapeDtypeStruct((self.nx * self.ny // 2, 2 * PAIR, self.r), BF)
        return [x, x, y, y, z, z]

    def slot(self, face, x, y, z):
        if face < 2:
            return (y, pl.ds(z * PAIR, PAIR))
        if face < 4:
            return (x, pl.ds(z * PAIR, PAIR))
        return (x * (self.ny // 2) + y // 2, pl.ds((y % 2) * PAIR, PAIR))

    def halo_faces(self, x_side, y, z):
        faces = [] if x_side is None else [x_side]
        if y == 0:
            faces.append(2)
        if y == self.ny - 1:
            faces.append(3)
        if z == 0:
            faces.append(4)
        if z == self.nz - 1:
            faces.append(5)
        return faces

    def work(self, x, x_side):
        return [
            (x * self.plane + y * self.nz + z, y, z, self.halo_faces(x_side, y, z))
            for y in range(self.ny)
            for z in range(self.nz)
        ]

    def of_planes(self, planes):
        return [(e, x, y, z, faces) for x, side in planes for e, y, z, faces in self.work(x, side)]

    def two_at_once(self, visit):
        lax.fori_loop(0, self.nx // 2, lambda i, carry: (visit([2 * i, 2 * i + 1]), carry)[1], 0)

    def every_plane(self, visit):
        lax.fori_loop(0, self.nx, lambda x, carry: (visit(x), carry)[1], 0)

    def inner_planes(self):
        return [(x, None) for x in range(1, self.nx - 1)]

    def end_planes(self):
        return [(0, 0), (self.nx - 1, 1)]

    def near_local(self, face, x, y, z):
        dx, dy, dz = [(-1, 0, 0), (1, 0, 0), (0, -1, 0), (0, 1, 0), (0, 0, -1), (0, 0, 1)][face]
        return (x + 1 + dx) * self.plane + (y + dy) * self.nz + (z + dz), face ^ 1


def even_in_z():
    return lax.rem(lax.axis_index("gz"), 2) == 0


def pick(near, f, place):
    if f < 4:
        return near[f][place]
    first, second = near[4][place], near[5][place]
    return jnp.where(even_in_z(), *((second, first) if f == 4 else (first, second)))


def send_traces(block, work, values, bt, sends):
    traces = [mm(jnp.concatenate([bt[f] for f in w[4]], axis=0), a).astype(BF) for w, a in zip(work, values)]
    low = None
    for (_, x, y, z, faces), t in zip(work, traces):
        for i, f in enumerate(faces):
            piece = t[i * PAD : i * PAD + PAIR]
            if f < 4:
                sends[f][block.slot(f, x, y, z)] = piece
            elif f == 4:
                low = piece
            else:
                sends[4][block.slot(4, x, y, z)] = jnp.where(even_in_z(), piece, low)
                sends[5][block.slot(4, x, y, z)] = jnp.where(even_in_z(), low, piece)


def first_sends(block, warm_start, a, trace_basis, bt):
    width = trace_basis.shape[-1]
    half = block.ny

    def along_x(w_ref, b_ref, low_ref, high_ref, w_buf, b_buf, sems):
        copies = [
            pltpu.make_async_copy(b_ref.at[pl.ds(0, 2)], b_buf, sems.at[0]),
            pltpu.make_async_copy(w_ref.at[pl.ds(0, half)], w_buf.at[pl.ds(0, half)], sems.at[1]),
            pltpu.make_async_copy(
                w_ref.at[pl.ds((block.nx - 1) * half, half)], w_buf.at[pl.ds(half, half)], sems.at[2]
            ),
        ]
        for copy in copies:
            copy.start()
        rows = lax.broadcasted_iota(jnp.int32, (block.c, block.nz * block.c), 0)
        cols = lax.broadcasted_iota(jnp.int32, (block.c, block.nz * block.c), 1)
        spread = [(cols == block.nz * rows + z).astype(BF) for z in range(block.nz)]
        none = jnp.zeros((PAD - width, block.c), BF)
        copies[0].wait()
        basis = [jnp.concatenate([b_buf[side], none], axis=0) for side in range(2)]
        wide = [
            jnp.concatenate([mm(basis[side], spread[z]).astype(BF) for z in range(block.nz)], axis=0)
            for side in range(2)
        ]
        for side, out_ref in enumerate((low_ref, high_ref)):
            copies[1 + side].wait()
            columns = [w_buf[side * half + y].reshape(block.nz * block.c, block.r) for y in range(half)]
            traces = [mm(wide[side], column).astype(BF) for column in columns]
            for y, t in enumerate(traces):
                for z in range(block.nz):
                    out_ref[block.slot(side, 0, y, z)] = t[z * PAD : z * PAD + PAIR]

    def others(a_ref, bt_ref, *sends):
        def visit(planes):
            work = block.of_planes([(x, None) for x in planes])
            send_traces(block, work, [a_ref[w[0]] for w in work], bt_ref, (None, None) + sends)

        block.two_at_once(visit)

    nx, ny, nz, c, r = warm_start.shape
    columns = warm_start.transpose(0, 1, 3, 2, 4).reshape(nx * ny, c, nz, r)
    shapes = block.send_shapes()
    scratch = [
        pltpu.VMEM((2 * ny, c, nz, r), BF),
        pltpu.VMEM((2, width, c), BF),
        pltpu.SemaphoreType.DMA((3,)),
    ]
    raw = [pltpu.with_memory_space_constraint(v, pltpu.HBM) for v in (columns, trace_basis.transpose(0, 2, 1))]
    first = call(along_x, shapes[:2], raw, FIRST, scratch, [HBM, HBM])
    return [*first, *call(others, shapes[2:], [a, bt], SECOND)]


def one_hots(o_ref, e):
    own = o_ref[e]
    group, modes = own.shape
    index = jnp.concatenate([own + v * modes for v in range(VARS)], axis=1)
    rows = lax.broadcasted_iota(jnp.int32, (PAD, VARS * modes), 0)
    return [(rows == index[f : f + 1]).astype(BF) for f in range(group)]


def prepared(block, jacobian, orientation, bt):
    count, group, width, _ = jacobian.shape
    many = 8

    def kernel(j_ref, o_ref, bt_ref, jp_ref, bc_ref, ball_ref):
        for f in range(group):
            basis = bt_ref[f].astype(F32).T.astype(BF)
            ball_ref[:, f * PAD : (f + 1) * PAD] = basis
            bc_ref[f] = jnp.concatenate([basis, jnp.zeros((block.c, LANES - PAD), BF)], axis=1)
        none = jnp.zeros((PAD - width, PAD), BF)

        def elements(step, carry):
            places = [many * step + i for i in range(many)]
            turned = [one_hots(o_ref, e) for e in places]
            moved = [
                [mm_t(j_ref[e, f], turn[f]).astype(BF) for f in range(group)]
                for e, turn in zip(places, turned)
            ]
            for e, values in zip(places, moved):
                for f in range(group):
                    jp_ref[e, f, :width] = values[f]
                    jp_ref[e, f, width:] = none
            return carry

        lax.fori_loop(0, count // many, elements, 0)

    shape = jax.ShapeDtypeStruct((count, group, PAD, PAD), BF)
    bc = jax.ShapeDtypeStruct((group, block.c, LANES), BF)
    ball = jax.ShapeDtypeStruct((block.c, group * PAD), BF)
    return call(kernel, [shape, bc, ball], [jacobian, orientation, bt], PREP)


def permutations(block, orientation, after):
    count, group, modes = orientation.shape

    def kernel(o_ref, _, p_ref):
        rows = lax.broadcasted_iota(jnp.int32, (PAD, VARS * modes), 0)
        eye = (rows == lax.broadcasted_iota(jnp.int32, (PAD, VARS * modes), 1)).astype(BF)

        def elements(step, carry):
            places = [8 * step + i for i in range(8)]
            values = [[mm_t(eye, turn).astype(BF) for turn in one_hots(o_ref, e)] for e in places]
            for e, value in zip(places, values):
                for f in range(group):
                    p_ref[e, f] = value[f]
            return carry

        lax.fori_loop(0, count // 8, elements, 0)

    shape = jax.ShapeDtypeStruct((count, group, PAD, PAD), BF)
    return call(kernel, shape, [orientation, after], PREP, specs=[VMEM, ANY])


def fill_traces(block, a_ref, bt_ref, t_ref):
    nx, plane = block.nx, block.plane
    t_ref[0:plane, 1] = jnp.zeros((plane, PAD, block.r), BF)
    t_ref[(nx + 1) * plane : (nx + 2) * plane, 0] = jnp.zeros((plane, PAD, block.r), BF)
    every = bt_ref[...].reshape(6 * PAD, block.c)

    def traces(x):
        t = []
        for i in range(0, plane, 2):
            pair = jnp.concatenate([a_ref[x * plane + i], a_ref[x * plane + i + 1]], axis=1)
            both = mm(every, pair).astype(BF)
            t += [both[:, : block.r], both[:, block.r :]]
        for i in range(plane):
            for f in range(6):
                t_ref[(x + 1) * plane + i, f] = t[i][f * PAD : (f + 1) * PAD]

    block.every_plane(traces)


def local_faces(block, y, z):
    return [f for f in range(6) if f < 2 or f not in block.halo_faces(None, y, z)]


def widened(pieces):
    gap = jnp.zeros((LANES - PAD, pieces[0].shape[1]), BF)
    return jnp.concatenate([part for p in pieces for part in (p, gap)], axis=0)


def coupled(bc_ref, faces, fluxes):
    return mm(jnp.concatenate([bc_ref[f] for f in faces], axis=1), widened(fluxes))


def local_residual(block, a, source, jp, bt, ball, after):
    def kernel(a_ref, s_ref, j_ref, bt_ref, ball_ref, *refs):
        r_ref, t_ref = refs[len(after) :]
        fill_traces(block, a_ref, bt_ref, t_ref)
        none = jnp.zeros((PAD, block.r), BF)

        def near_fluxes(j_ref, e, x, y, z, faces):
            fluxes = []
            for i in range(0, len(faces), 2):
                some = faces[i : i + 2]
                near = jnp.concatenate([t_ref[block.near_local(f, x, y, z)] for f in some], axis=1)
                both = mm(jnp.concatenate([j_ref[e, f] for f in some], axis=0), near).astype(BF)
                for k in range(len(some)):
                    fluxes.append(both[k * PAD : (k + 1) * PAD, k * block.r : (k + 1) * block.r])
            return fluxes

        def planes(step, carry):
            work = [
                (e, x, y, z, local_faces(block, y, z))
                for x in (2 * step, 2 * step + 1)
                for e, y, z, _ in block.work(x, None)
            ]
            full = []
            for e, x, y, z, faces in work:
                fluxes = dict(zip(faces, near_fluxes(j_ref, e, x, y, z, faces)))
                full.append(jnp.concatenate([fluxes.get(f, none) for f in range(6)], axis=0))
            rest = []
            for i in range(0, len(work), 2):
                both = mm(ball_ref[...], jnp.concatenate(full[i : i + 2], axis=1))
                rest += [both[:, : block.r], both[:, block.r :]]
            for w, value in zip(work, rest):
                r_ref[w[0]] = s_ref[w[0]].astype(F32) - value
            return carry

        lax.fori_loop(0, block.nx // 2, planes, 0)

    count = block.nx * block.plane
    traces = pltpu.VMEM(((block.nx + 2) * block.plane, 6, PAD, block.r), BF)
    shape = jax.ShapeDtypeStruct((count, block.c, block.r), F32)
    operands = [a, source, jp, bt, ball, *after]
    return call(kernel, shape, operands, LOCAL, [traces], [VMEM] * 5 + [ANY] * len(after))


def z_then_y(parts):
    return [*parts[4:], *parts[2:4]]


def by_face(refs):
    return (None, None) + tuple(refs[2:4]) + tuple(refs[:2])


def x_fluxes(block, halos, jp):
    def kernel(low_ref, high_ref, j_ref, out_ref):
        near = (low_ref, high_ref)
        fluxes = [
            mm(j_ref[e, side, :, :PAIR], near[side][block.slot(side, x, y, z)]).astype(BF)
            for x, side in block.end_planes()
            for e, y, z, _ in block.work(x, None)
        ]
        for i, flux in enumerate(fluxes):
            out_ref[i] = flux

    shape = jax.ShapeDtypeStruct((2 * block.plane, PAD, block.r), BF)
    return call(kernel, shape, [*halos, jp], WAIT)


def finish_sweep(block, halos, residual, inverse, jp, bt, bc):
    def finish(work, ready, near, r_ref, v_ref, j_ref, bc_ref):
        fluxes = [
            [
                ready[i]
                if f < 2
                else mm(j_ref[e, f, :, :PAIR], pick(near, f, block.slot(f, x, y, z))).astype(BF)
                for f in faces
            ]
            for i, (e, x, y, z, faces) in enumerate(work)
        ]
        rest = [(r_ref[w[0]] - coupled(bc_ref, w[4], flux)).astype(BF) for w, flux in zip(work, fluxes)]
        return [mm(v_ref[w[0]], value).astype(BF) for w, value in zip(work, rest)]

    def write(work, values, bt_ref, sends, a_ref):
        send_traces(block, work, values, bt_ref, sends)
        for w, value in zip(work, values):
            a_ref[w[0]] = value

    def ends(*refs):
        ready, near, fixed, (bt_ref, a_ref, *sends) = refs[0], by_face(refs[1:5]), refs[5:9], refs[9:]
        work = block.of_planes(block.end_planes())
        values = finish(work, ready, near, *fixed)
        write([(e, x, y, z, faces[:1]) for e, x, y, z, faces in work], values, bt_ref, sends, a_ref)

    def inner(*refs):
        done_ref, near, fixed, (bt_ref, a_ref, *sends) = refs[0], by_face(refs[1:5]), refs[5:9], refs[9:]
        work = block.of_planes(block.inner_planes())
        outer = block.of_planes([(x, None) for x, _ in block.end_planes()])
        values = finish(work, None, near, *fixed)
        write(work + outer, values + [done_ref[w[0]] for w in outer], bt_ref, [None, None, *sends], a_ref)

    fixed = [residual, inverse, jp, bc, bt]
    shapes = block.send_shapes()
    whole = jax.ShapeDtypeStruct((block.nx * block.plane, block.c, block.r), BF)
    ready = x_fluxes(block, halos[:2], jp)
    part, *sends = call(ends, [whole] + shapes[:2], [ready, *z_then_y(halos), *fixed], FIRST)
    a, *rest = call(inner, [whole] + shapes[2:], [part, *z_then_y(halos), *fixed], SECOND)
    return a, [*sends, *rest]


def local_gradient(block, a, jp, p, bt, after):
    def kernel(a_ref, j_ref, p_ref, bt_ref, _, g_ref, t_ref):
        fill_traces(block, a_ref, bt_ref, t_ref)

        def plane(x, carry):
            grads = []
            for e, y, z, _ in block.work(x, None):
                rows = [jnp.zeros((1, block.r), F32)] * 8
                for f in local_faces(block, y, z):
                    both = jnp.concatenate([j_ref[e, f], p_ref[e, f]], axis=0)
                    both = mm(both, t_ref[block.near_local(f, x, y, z)])
                    own = t_ref[e + block.plane, f].astype(F32)
                    rows[f] = jnp.sum((own - both[PAD:]) * both[:PAD], axis=0, keepdims=True)
                grads.append((e, jnp.concatenate(rows, axis=0)))
            for e, value in grads:
                g_ref[e] = value
            return carry

        lax.fori_loop(0, block.nx, plane, 0)

    count = block.nx * block.plane
    return call(
        kernel,
        jax.ShapeDtypeStruct((count, 8, block.r), F32),
        [a, jp, p, bt, after],
        LOCAL,
        [pltpu.VMEM(((block.nx + 2) * block.plane, 6, PAD, block.r), BF)],
        [VMEM] * 4 + [ANY],
    )


def finish_gradient(block, halos, owns, inside, jp, p):
    def add(work, near, own, j_ref, p_ref, g_ref):
        total = []
        for e, x, y, z, faces in work:
            rows = [jnp.zeros((1, block.r), F32)] * 8
            for f in faces:
                place = block.slot(f, x, y, z)
                both = jnp.concatenate([j_ref[e, f, :, :PAIR], p_ref[e, f, :, :PAIR]], axis=0)
                both = mm(both, pick(near, f, place))
                gap = pick(own, f, place).astype(F32) - both[PAD : PAD + PAIR]
                rows[f] = jnp.sum(gap * both[:PAIR], axis=0, keepdims=True)
            total.append(g_ref[e] + jnp.concatenate(rows, axis=0))
        return total

    def along_x(*refs):
        near, own, (j_ref, p_ref, g_ref, out_ref) = refs[:2], refs[2:4], refs[4:]

        for x, side in block.end_planes():
            work = [(e, x, y, z, [side]) for e, y, z, _ in block.work(x, None)]
            for w, value in zip(work, add(work, near, own, j_ref, p_ref, g_ref)):
                out_ref[w[0]] = value
        kept = slice(block.plane, (block.nx - 1) * block.plane)
        out_ref[kept] = g_ref[kept]

    def others(*refs):
        near, own, (j_ref, p_ref, g_ref, out_ref) = by_face(refs[:4]), by_face(refs[4:8]), refs[8:]

        def visit(planes):
            work = block.of_planes([(x, None) for x in planes])
            total = add(work, near, own, j_ref, p_ref, g_ref)
            for i in range(0, len(work), block.nz):
                _, x, y, _, _ = work[i]
                for f in range(6):
                    rows = [g[f : f + 1] for g in total[i : i + block.nz]]
                    out_ref[x * block.ny + y, f] = jnp.concatenate(rows, axis=0)

        block.two_at_once(visit)

    inside = call(along_x, inside, [*halos[:2], *owns[:2], jp, p, inside], WAIT)
    shape = jax.ShapeDtypeStruct((block.nx * block.ny, 6, block.nz, block.r), F32)
    return call(others, shape, [*z_then_y(halos), *z_then_y(owns), jp, p, inside], LOCAL)


def exchange(sends):
    halos = []
    for d, axis in enumerate(("gx", "gy")):
        count = lax.axis_size(axis)
        up = [(i, (i + 1) % count) for i in range(count)]
        down = [(j, i) for i, j in up]
        halos.append(lax.ppermute(sends[2 * d + 1], axis, up))
        halos.append(lax.ppermute(sends[2 * d], axis, down))
    for part, start in enumerate((0, 1)):
        pairs = [(i, i + 1) for i in range(start, lax.axis_size("gz") - 1, 2)]
        halos.append(lax.ppermute(sends[4 + part], "gz", pairs + [(j, i) for i, j in pairs]))
    return halos


def on_device(adjoint_source, warm_start, block_inverse, face_jacobian, trace_basis, orientation):
    nx, ny, nz, c, r = warm_start.shape
    count = nx * ny * nz
    width = trace_basis.shape[-1]
    modes = orientation.shape[-1]
    block = Block(nx, ny, nz, c, r)
    gap = PAD - width

    bt = jnp.pad(trace_basis.transpose(0, 2, 1), ((0, 0), (0, gap), (0, 0)))
    adjoint = warm_start.reshape(count, c, r)
    sends = first_sends(block, warm_start, adjoint, trace_basis, bt)

    source = adjoint_source.reshape(count, c, r)
    inverse = block_inverse.reshape(count, c, c)
    turns = orientation.reshape(count, 6, modes)
    jacobian = face_jacobian.reshape(count, 6, width, width)
    jp, bc, ball = prepared(block, jacobian, turns, bt)

    for sweep in range(SWEEPS):
        halos = exchange(sends)
        after = [halos[0]]
        if sweep == SWEEPS - 1:
            p = permutations(block, turns, adjoint)
            after.append(p)
        residual = local_residual(block, adjoint, source, jp, bt, ball, after)
        if sweep == 0:
            inverse, residual = lax.optimization_barrier((block_inverse, residual))
            inverse = inverse.reshape(count, c, c)
        adjoint, sends = finish_sweep(block, halos, residual, inverse, jp, bt, bc)
    halos = exchange(sends)
    inside = local_gradient(block, adjoint, jp, p, bt, halos[0])
    gradient = finish_gradient(block, halos, sends, inside, jp, p)
    gradient = gradient.reshape(nx, ny, 6, nz, r).transpose(0, 1, 3, 2, 4)
    return (adjoint.reshape(warm_start.shape), gradient)


def solution(mesh):
    return jax.shard_map(
        on_device,
        mesh=mesh,
        in_specs=(
            P("gx", "gy", "gz", None, None),
            P("gx", "gy", "gz", None, None),
            P("gx", "gy", "gz", None, None),
            P("gx", "gy", "gz", None, None, None),
            P(),
            P("gx", "gy", "gz", None, None),
        ),
        out_specs=(P("gx", "gy", "gz", None, None), P("gx", "gy", "gz", None, None)),
        check_vma=False,
    )
```

```python
import jax
import jax.numpy as jnp
from jax import lax
from jax.experimental import pallas as pl
from jax.experimental.pallas import tpu as pltpu
from jax.sharding import PartitionSpec as P

SWEEPS = 2
VARS = 5
FIRST = 1000
SECOND = 1000
LOCAL = 1000
PREP = 1000
WAIT = 2500000000
WAIT_Z = 2500000000
PAIR = 76
PAD = 80
LANES = 128
BF = jnp.bfloat16
F32 = jnp.float32
MIB = 1024 * 1024
VMEM = pl.BlockSpec(memory_space=pltpu.VMEM)
ANY = pl.BlockSpec(memory_space=pl.ANY)
HBM = pl.BlockSpec(memory_space=pltpu.HBM)


def mm(a, b):
    return jnp.dot(a, b, preferred_element_type=F32)


def mm_t(a, b):
    return lax.dot_general(a, b, (((1,), (1,)), ((), ())), preferred_element_type=F32)


def call(kernel, out_shape, operands, flops, scratch=(), specs=None, outs=None, vmem=12):
    return pl.pallas_call(
        kernel,
        out_shape=out_shape,
        in_specs=specs or [VMEM] * len(operands),
        out_specs=outs or jax.tree.map(lambda _: VMEM, out_shape),
        scratch_shapes=list(scratch),
        compiler_params=pltpu.CompilerParams(vmem_limit_bytes=vmem * MIB),
        cost_estimate=pl.CostEstimate(flops=flops, bytes_accessed=0, transcendentals=0),
    )(*operands)


class Block:
    def __init__(self, nx, ny, nz, c, r, split=False):
        self.split = split
        self.nx, self.ny, self.nz, self.c, self.r = nx, ny, nz, c, r
        self.plane = ny * nz

    def parted(self):
        return Block(self.nx, self.ny, self.nz, self.c, self.r, True)

    def send_shapes(self):
        rows = self.nz * PAIR
        x = jax.ShapeDtypeStruct((self.ny, rows, self.r), BF)
        y = jax.ShapeDtypeStruct((self.nx, rows, self.r), BF)
        planes = [2, 2, self.nx - 2, self.nx - 2] if self.split else [self.nx] * 2
        z = [jax.ShapeDtypeStruct((n * self.ny // 2, 2 * PAIR, self.r), BF) for n in planes]
        return [x, x, y, y, *z]

    def z_buffers(self, x):
        return (6, 7) if self.split and 0 < x < self.nx - 1 else (4, 5)

    def slot(self, face, x, y, z):
        if face < 2:
            return (y, pl.ds(z * PAIR, PAIR))
        if face < 4:
            return (x, pl.ds(z * PAIR, PAIR))
        plane = {0: 0, self.nx - 1: 1}.get(x, x - 1) if self.split else x
        return (plane * (self.ny // 2) + y // 2, pl.ds((y % 2) * PAIR, PAIR))

    def halo_faces(self, x_side, y, z):
        faces = [] if x_side is None else [x_side]
        if y == 0:
            faces.append(2)
        if y == self.ny - 1:
            faces.append(3)
        if z == 0:
            faces.append(4)
        if z == self.nz - 1:
            faces.append(5)
        return faces

    def work(self, x, x_side):
        return [
            (x * self.plane + y * self.nz + z, y, z, self.halo_faces(x_side, y, z))
            for y in range(self.ny)
            for z in range(self.nz)
        ]

    def of_planes(self, planes):
        return [(e, x, y, z, faces) for x, side in planes for e, y, z, faces in self.work(x, side)]

    def two_at_once(self, visit):
        lax.fori_loop(0, self.nx // 2, lambda i, carry: (visit([2 * i, 2 * i + 1]), carry)[1], 0)

    def every_plane(self, visit):
        lax.fori_loop(0, self.nx, lambda x, carry: (visit(x), carry)[1], 0)

    def inner_planes(self):
        return [(x, None) for x in range(1, self.nx - 1)]

    def end_planes(self):
        return [(0, 0), (self.nx - 1, 1)]

    def near_local(self, face, x, y, z):
        dx, dy, dz = [(-1, 0, 0), (1, 0, 0), (0, -1, 0), (0, 1, 0), (0, 0, -1), (0, 0, 1)][face]
        return (x + 1 + dx) * self.plane + (y + dy) * self.nz + (z + dz), face ^ 1


def even_in_z():
    return lax.rem(lax.axis_index("gz"), 2) == 0


def pick(block, near, f, x, y, z):
    place = block.slot(f, x, y, z)
    if f < 4:
        return near[f][place]
    first, second = (near[i][place] for i in block.z_buffers(x))
    return jnp.where(even_in_z(), *((second, first) if f == 4 else (first, second)))


def send_traces(block, work, values, bt, sends):
    traces = [mm(jnp.concatenate([bt[f] for f in w[4]], axis=0), a).astype(BF) for w, a in zip(work, values)]
    low = None
    for (_, x, y, z, faces), t in zip(work, traces):
        for i, f in enumerate(faces):
            piece = t[i * PAD : i * PAD + PAIR]
            if f < 4:
                sends[f][block.slot(f, x, y, z)] = piece
            elif f == 4:
                low = piece
            else:
                first, second = (sends[i] for i in block.z_buffers(x))
                first[block.slot(4, x, y, z)] = jnp.where(even_in_z(), piece, low)
                second[block.slot(4, x, y, z)] = jnp.where(even_in_z(), low, piece)


def only(work, faces):
    return [(*w[:4], [f for f in w[4] if f in faces]) for w in work]


X, Y, Z = (0, 1), (2, 3), (4, 5)


def first_sends(block, warm_start, a, trace_basis, bt):
    width = trace_basis.shape[-1]
    half = block.ny

    def along_x(w_ref, b_ref, low_ref, high_ref, w_buf, b_buf, sems):
        copies = [
            pltpu.make_async_copy(b_ref.at[pl.ds(0, 2)], b_buf, sems.at[0]),
            pltpu.make_async_copy(w_ref.at[pl.ds(0, half)], w_buf.at[pl.ds(0, half)], sems.at[1]),
            pltpu.make_async_copy(
                w_ref.at[pl.ds((block.nx - 1) * half, half)], w_buf.at[pl.ds(half, half)], sems.at[2]
            ),
        ]
        for copy in copies:
            copy.start()
        rows = lax.broadcasted_iota(jnp.int32, (block.c, block.nz * block.c), 0)
        cols = lax.broadcasted_iota(jnp.int32, (block.c, block.nz * block.c), 1)
        spread = [(cols == block.nz * rows + z).astype(BF) for z in range(block.nz)]
        none = jnp.zeros((PAD - width, block.c), BF)
        copies[0].wait()
        basis = [jnp.concatenate([b_buf[side], none], axis=0) for side in range(2)]
        wide = [
            jnp.concatenate([mm(basis[side], spread[z]).astype(BF) for z in range(block.nz)], axis=0)
            for side in range(2)
        ]
        for side, out_ref in enumerate((low_ref, high_ref)):
            copies[1 + side].wait()
            columns = [w_buf[side * half + y].reshape(block.nz * block.c, block.r) for y in range(half)]
            traces = [mm(wide[side], column).astype(BF) for column in columns]
            for y, t in enumerate(traces):
                for z in range(block.nz):
                    out_ref[block.slot(side, 0, y, z)] = t[z * PAD : z * PAD + PAIR]

    def others(a_ref, bt_ref, *sends):
        def visit(planes):
            work = block.of_planes([(x, None) for x in planes])
            send_traces(block, work, [a_ref[w[0]] for w in work], bt_ref, (None, None) + sends)

        block.two_at_once(visit)

    nx, ny, nz, c, r = warm_start.shape
    columns = warm_start.transpose(0, 1, 3, 2, 4).reshape(nx * ny, c, nz, r)
    shapes = block.send_shapes()
    scratch = [
        pltpu.VMEM((2 * ny, c, nz, r), BF),
        pltpu.VMEM((2, width, c), BF),
        pltpu.SemaphoreType.DMA((3,)),
    ]
    raw = [pltpu.with_memory_space_constraint(v, pltpu.HBM) for v in (columns, trace_basis.transpose(0, 2, 1))]
    first = call(along_x, shapes[:2], raw, FIRST, scratch, [HBM, HBM])
    return [*first, *call(others, shapes[2:], [a, bt], SECOND)]


def one_hots(o_ref, e):
    own = o_ref[e]
    group, modes = own.shape
    index = jnp.concatenate([own + v * modes for v in range(VARS)], axis=1)
    rows = lax.broadcasted_iota(jnp.int32, (PAD, VARS * modes), 0)
    return [(rows == index[f : f + 1]).astype(BF) for f in range(group)]


def prepared(block, jacobian, orientation, bt):
    count, group, width, _ = jacobian.shape
    many = 8

    def kernel(j_ref, o_ref, bt_ref, jp_ref, p_ref, bc_ref, ball_ref):
        for f in range(group):
            basis = bt_ref[f].astype(F32).T.astype(BF)
            ball_ref[:, f * PAD : (f + 1) * PAD] = basis
            bc_ref[f] = jnp.concatenate([basis, jnp.zeros((block.c, LANES - PAD), BF)], axis=1)
        none = jnp.zeros((PAD - width, PAD), BF)
        rows = lax.broadcasted_iota(jnp.int32, (PAD, width), 0)
        eye = (rows == lax.broadcasted_iota(jnp.int32, (PAD, width), 1)).astype(BF)

        def elements(step, carry):
            places = [many * step + i for i in range(many)]
            turned = [one_hots(o_ref, e) for e in places]
            moved = [
                [mm_t(j_ref[e, f], turn[f]).astype(BF) for f in range(group)]
                for e, turn in zip(places, turned)
            ]
            placed = [[mm_t(eye, turn[f]).astype(BF) for f in range(group)] for turn in turned]
            for e, values, perms in zip(places, moved, placed):
                for f in range(group):
                    p_ref[e, f] = perms[f]
                    jp_ref[e, f, :width] = values[f]
                    jp_ref[e, f, width:] = none
            return carry

        lax.fori_loop(0, count // many, elements, 0)

    shape = jax.ShapeDtypeStruct((count, group, PAD, PAD), BF)
    bc = jax.ShapeDtypeStruct((group, block.c, LANES), BF)
    ball = jax.ShapeDtypeStruct((block.c, group * PAD), BF)
    return call(kernel, [shape, shape, bc, ball], [jacobian, orientation, bt], PREP)


def fill_traces(block, a_ref, bt_ref, t_ref):
    nx, plane = block.nx, block.plane
    t_ref[0:plane, 1] = jnp.zeros((plane, PAD, block.r), BF)
    t_ref[(nx + 1) * plane : (nx + 2) * plane, 0] = jnp.zeros((plane, PAD, block.r), BF)
    every = bt_ref[...].reshape(6 * PAD, block.c)

    def traces(x):
        t = []
        for i in range(0, plane, 2):
            pair = jnp.concatenate([a_ref[x * plane + i], a_ref[x * plane + i + 1]], axis=1)
            both = mm(every, pair).astype(BF)
            t += [both[:, : block.r], both[:, block.r :]]
        for i in range(plane):
            for f in range(6):
                t_ref[(x + 1) * plane + i, f] = t[i][f * PAD : (f + 1) * PAD]

    block.every_plane(traces)


def local_faces(block, y, z):
    return [f for f in range(6) if f < 2 or f not in block.halo_faces(None, y, z)]


def widened(pieces):
    gap = jnp.zeros((LANES - PAD, pieces[0].shape[1]), BF)
    return jnp.concatenate([part for p in pieces for part in (p, gap)], axis=0)


def coupled(bc_ref, faces, fluxes):
    return mm(jnp.concatenate([bc_ref[f] for f in faces], axis=1), widened(fluxes))


def local_residual(block, a, source, jp, bt, ball, after):
    def kernel(a_ref, s_ref, j_ref, bt_ref, ball_ref, *refs):
        r_ref, t_ref = refs[len(after) :]
        fill_traces(block, a_ref, bt_ref, t_ref)
        none = jnp.zeros((PAD, block.r), BF)

        def near_fluxes(j_ref, e, x, y, z, faces):
            fluxes = []
            for i in range(0, len(faces), 2):
                some = faces[i : i + 2]
                near = jnp.concatenate([t_ref[block.near_local(f, x, y, z)] for f in some], axis=1)
                both = mm(jnp.concatenate([j_ref[e, f] for f in some], axis=0), near).astype(BF)
                for k in range(len(some)):
                    fluxes.append(both[k * PAD : (k + 1) * PAD, k * block.r : (k + 1) * block.r])
            return fluxes

        def planes(step, carry):
            work = [
                (e, x, y, z, local_faces(block, y, z))
                for x in (2 * step, 2 * step + 1)
                for e, y, z, _ in block.work(x, None)
            ]
            full = []
            for e, x, y, z, faces in work:
                fluxes = dict(zip(faces, near_fluxes(j_ref, e, x, y, z, faces)))
                full.append(jnp.concatenate([fluxes.get(f, none) for f in range(6)], axis=0))
            rest = []
            for i in range(0, len(work), 2):
                both = mm(ball_ref[...], jnp.concatenate(full[i : i + 2], axis=1))
                rest += [both[:, : block.r], both[:, block.r :]]
            for w, value in zip(work, rest):
                r_ref[w[0]] = s_ref[w[0]].astype(F32) - value
            return carry

        lax.fori_loop(0, block.nx // 2, planes, 0)

    count = block.nx * block.plane
    traces = pltpu.VMEM(((block.nx + 2) * block.plane, 6, PAD, block.r), BF)
    shape = jax.ShapeDtypeStruct((count, block.c, block.r), F32)
    operands = [a, source, jp, bt, ball, *after]
    return call(kernel, shape, operands, LOCAL, [traces], [VMEM] * 5 + [ANY] * len(after))


def z_then_y(parts):
    return [*parts[4:], *parts[2:4]]


def by_face(refs):
    return (None, None) + tuple(refs[2:4]) + tuple(refs[:2])


def z_fluxes(block, halos, jp, after):
    def kernel(first_ref, second_ref, j_ref, _, out_ref):
        near = [None] * 4 + [first_ref, second_ref]
        work = only(block.of_planes(block.end_planes()), Z)
        fluxes = [mm(j_ref[e, f[0], :, :PAIR], pick(block, near, f[0], x, y, z)).astype(BF) for e, x, y, z, f in work]
        for i, flux in enumerate(fluxes):
            out_ref[i] = flux

    shape = jax.ShapeDtypeStruct((2 * block.plane, PAD, block.r), BF)
    return call(kernel, shape, [*halos, jp, after], WAIT_Z, specs=[VMEM, VMEM, VMEM, ANY])


def x_fluxes(block, halos, jp, along_z=()):
    count = 2 * block.plane

    def kernel(low_ref, high_ref, j_ref, *refs):
        near = (low_ref, high_ref)
        work = only(block.of_planes(block.end_planes()), X)
        fluxes = [mm(j_ref[e, f[0], :, :PAIR], pick(block, near, f[0], x, y, z)).astype(BF) for e, x, y, z, f in work]
        for i, flux in enumerate(fluxes):
            refs[-1][i] = flux
        for ref in refs[:-1]:
            refs[-1][count:] = ref[...]

    shape = jax.ShapeDtypeStruct((count * (1 + len(along_z)), PAD, block.r), BF)
    return call(kernel, shape, [*halos, jp, *along_z], WAIT)


def finish_sweep(block, later, halos, residual, inverse, jp, bt, bc):
    def finish(work, ready, near, r_ref, v_ref, j_ref, bc_ref):
        def flux(i, e, x, y, z, f):
            if f in X:
                return ready[i]
            if ready is not None and block.split and f in Z:
                return ready[2 * block.plane + i]
            return mm(j_ref[e, f, :, :PAIR], pick(block, near, f, x, y, z)).astype(BF)

        fluxes = [[flux(i, e, x, y, z, f) for f in faces] for i, (e, x, y, z, faces) in enumerate(work)]
        rest = [(r_ref[w[0]] - coupled(bc_ref, w[4], flux)).astype(BF) for w, flux in zip(work, fluxes)]
        return [mm(v_ref[w[0]], value).astype(BF) for w, value in zip(work, rest)]

    first = X + Z if later.split else X

    def ends(*refs):
        count = 2 if block.split else 4
        ready, near, refs = refs[0], (None, None, *refs[1 : 1 + count]), refs[1 + count :]
        fixed, (bt_ref, a_ref, *sends) = refs[:4], refs[4:]
        work = block.of_planes(block.end_planes())
        values = finish(work, ready, near, *fixed)
        send_traces(later, only(work, first), values, bt_ref, [*sends[:2], None, None, *sends[2:]])
        for w, value in zip(work, values):
            a_ref[w[0]] = value

    def inner(*refs):
        done_ref, fixed, (bt_ref, a_ref, *sends) = refs[0], refs[5:9], refs[9:]
        near = (None, None, *refs[1:3], *((None, None) if block.split else ()), *refs[3:5])
        sends = [None, None, *sends[:2], *((None, None) if later.split else ()), *sends[2:]]
        work = block.of_planes(block.inner_planes())
        outer = [(*w, done_ref[w[0]]) for w in block.of_planes(block.end_planes())]
        values = finish(work, None, near, *fixed)
        passed = only(outer, [f for f in range(6) if f not in first])
        passed = [(w, o[5]) for w, o in zip(passed, outer) if w[4]]
        send_traces(later, work, values, bt_ref, sends)
        send_traces(later, [w for w, _ in passed], [v for _, v in passed], bt_ref, sends)
        for w, value in zip(work, values):
            a_ref[w[0]] = value
        for w in outer:
            a_ref[w[0]] = w[5]

    fixed = [residual, inverse, jp, bc, bt]
    shapes = later.send_shapes()
    whole = jax.ShapeDtypeStruct((block.nx * block.plane, block.c, block.r), BF)
    early = [z_fluxes(block, halos[4:6], jp, residual)] if block.split else []
    ready = x_fluxes(block, halos[:2], jp, early)
    z = [] if block.split else halos[4:]
    leaving = shapes[:2] + (shapes[4:6] if later.split else [])
    part, *lead = call(ends, [whole] + leaving, [ready, *halos[2:4], *z, *fixed], FIRST)
    operands = [part, *halos[2:4], *halos[-2:], *fixed]
    a, *rest = call(inner, [whole] + shapes[2:4] + shapes[-2:], operands, SECOND)
    return a, [*lead[:2], *rest[:2], *lead[2:], *rest[2:]]


def local_gradient(block, a, jp, p, bt, after):
    columns = a.reshape(block.nx * block.ny, block.nz, block.c, block.r).transpose(0, 2, 1, 3)

    def kernel(a_ref, w_ref, j_ref, p_ref, bt_ref, _, g_ref, out_ref, t_ref, sem):
        leave = pltpu.make_async_copy(w_ref, out_ref, sem)
        leave.start()
        fill_traces(block, a_ref, bt_ref, t_ref)

        def plane(x, carry):
            grads = []
            for e, y, z, _ in block.work(x, None):
                rows = [jnp.zeros((1, block.r), F32)] * 8
                for f in local_faces(block, y, z):
                    both = jnp.concatenate([j_ref[e, f], p_ref[e, f]], axis=0)
                    both = mm(both, t_ref[block.near_local(f, x, y, z)])
                    own = t_ref[e + block.plane, f].astype(F32)
                    rows[f] = jnp.sum((own - both[PAD:]) * both[:PAD], axis=0, keepdims=True)
                grads.append((e, jnp.concatenate(rows, axis=0)))
            for e, value in grads:
                g_ref[e] = value
            return carry

        lax.fori_loop(0, block.nx, plane, 0)
        leave.wait()

    count = block.nx * block.plane
    shapes = [jax.ShapeDtypeStruct((count, 8, block.r), F32), jax.ShapeDtypeStruct(columns.shape, BF)]
    scratch = [
        pltpu.VMEM(((block.nx + 2) * block.plane, 6, PAD, block.r), BF),
        pltpu.SemaphoreType.DMA(()),
    ]
    operands = [a, columns, jp, p, bt, after]
    return call(kernel, shapes, operands, LOCAL, scratch, [VMEM] * 5 + [ANY], outs=[VMEM, HBM])


def finish_gradient(block, halos, owns, inside, jp, p):
    def add(work, near, own, j_ref, p_ref, g_ref):
        total = []
        for e, x, y, z, faces in work:
            rows = [jnp.zeros((1, block.r), F32)] * 8
            for f in faces:
                both = jnp.concatenate([j_ref[e, f, :, :PAIR], p_ref[e, f, :, :PAIR]], axis=0)
                both = mm(both, pick(block, near, f, x, y, z))
                gap = pick(block, own, f, x, y, z).astype(F32) - both[PAD : PAD + PAIR]
                rows[f] = jnp.sum(gap * both[:PAIR], axis=0, keepdims=True)
            total.append(g_ref[e] + jnp.concatenate(rows, axis=0))
        return total

    def along_x(*refs):
        near, own, (j_ref, p_ref, g_ref, out_ref) = refs[:2], refs[2:4], refs[4:]

        for x, side in block.end_planes():
            work = [(e, x, y, z, [side]) for e, y, z, _ in block.work(x, None)]
            for w, value in zip(work, add(work, near, own, j_ref, p_ref, g_ref)):
                out_ref[w[0]] = value
        kept = slice(block.plane, (block.nx - 1) * block.plane)
        out_ref[kept] = g_ref[kept]

    def others(*refs):
        near, own, (j_ref, p_ref, g_ref, out_ref) = by_face(refs[:4]), by_face(refs[4:8]), refs[8:]

        def visit(planes):
            work = block.of_planes([(x, None) for x in planes])
            total = add(work, near, own, j_ref, p_ref, g_ref)
            for i in range(0, len(work), block.nz):
                _, x, y, _, _ = work[i]
                for f in range(6):
                    rows = [g[f : f + 1] for g in total[i : i + block.nz]]
                    out_ref[x * block.ny + y, f] = jnp.concatenate(rows, axis=0)

        block.two_at_once(visit)

    inside = call(along_x, inside, [*halos[:2], *owns[:2], jp, p, inside], WAIT)
    shape = jax.ShapeDtypeStruct((block.nx * block.ny, 6, block.nz, block.r), F32)
    return call(others, shape, [*z_then_y(halos), *z_then_y(owns), jp, p, inside], LOCAL)


def exchange(sends):
    halos = []
    for d, axis in enumerate(("gx", "gy")):
        count = lax.axis_size(axis)
        up = [(i, (i + 1) % count) for i in range(count)]
        down = [(j, i) for i, j in up]
        halos.append(lax.ppermute(sends[2 * d + 1], axis, up))
        halos.append(lax.ppermute(sends[2 * d], axis, down))
    for i in range(4, len(sends)):
        pairs = [(j, j + 1) for j in range(i % 2, lax.axis_size("gz") - 1, 2)]
        halos.append(lax.ppermute(sends[i], "gz", pairs + [(k, j) for j, k in pairs]))
    return halos


def on_device(adjoint_source, warm_start, block_inverse, face_jacobian, trace_basis, orientation):
    nx, ny, nz, c, r = warm_start.shape
    count = nx * ny * nz
    width = trace_basis.shape[-1]
    modes = orientation.shape[-1]
    block = Block(nx, ny, nz, c, r)
    gap = PAD - width

    bt = jnp.pad(trace_basis.transpose(0, 2, 1), ((0, 0), (0, gap), (0, 0)))
    adjoint = warm_start.reshape(count, c, r)
    sends = first_sends(block, warm_start, adjoint, trace_basis, bt)

    source = adjoint_source.reshape(count, c, r)
    inverse = block_inverse.reshape(count, c, c)
    turns = orientation.reshape(count, 6, modes)
    jacobian = face_jacobian.reshape(count, 6, width, width)
    jp, p, bc, ball = prepared(block, jacobian, turns, bt)

    parted = block.parted()
    for sweep in range(SWEEPS):
        halos = exchange(sends)
        now, later = (block, parted) if sweep == 0 else (parted, block)
        after = [halos[0] if sweep == 0 else halos[4]]
        residual = local_residual(block, adjoint, source, jp, bt, ball, after)
        if sweep == 0:
            inverse, residual = lax.optimization_barrier((block_inverse, residual))
            inverse = inverse.reshape(count, c, c)
        adjoint, sends = finish_sweep(now, later, halos, residual, inverse, jp, bt, bc)
    halos = exchange(sends)
    inside, adjoint = local_gradient(block, adjoint, jp, p, bt, halos[0])
    adjoint = adjoint.reshape(nx, ny, c, nz, r).transpose(0, 1, 3, 2, 4)
    gradient = finish_gradient(block, halos, sends, inside, jp, p)
    gradient = gradient.reshape(nx, ny, 6, nz, r).transpose(0, 1, 3, 2, 4)
    return (adjoint, gradient)


def solution(mesh):
    return jax.shard_map(
        on_device,
        mesh=mesh,
        in_specs=(
            P("gx", "gy", "gz", None, None),
            P("gx", "gy", "gz", None, None),
            P("gx", "gy", "gz", None, None),
            P("gx", "gy", "gz", None, None, None),
            P(),
            P("gx", "gy", "gz", None, None),
        ),
        out_specs=(P("gx", "gy", "gz", None, None), P("gx", "gy", "gz", None, None)),
        check_vma=False,
    )
```

```python
import jax
import jax.numpy as jnp
from jax import lax
from jax.experimental import pallas as pl
from jax.experimental.pallas import tpu as pltpu
from jax.sharding import PartitionSpec as P

SWEEPS = 2
VARS = 5
FIRST = 1000
SECOND = 1000
LOCAL = 1000
PREP = 1000
WAIT = 2500000000
WAIT_Z = 2500000000
PAIR = 76
PAD = 80
LANES = 128
BF = jnp.bfloat16
F32 = jnp.float32
MIB = 1024 * 1024
VMEM = pl.BlockSpec(memory_space=pltpu.VMEM)
ANY = pl.BlockSpec(memory_space=pl.ANY)
HBM = pl.BlockSpec(memory_space=pltpu.HBM)


def mm(a, b):
    return jnp.dot(a, b, preferred_element_type=F32)


def mm_t(a, b):
    return lax.dot_general(a, b, (((1,), (1,)), ((), ())), preferred_element_type=F32)


def call(kernel, out_shape, operands, flops, scratch=(), specs=None, outs=None, vmem=12):
    return pl.pallas_call(
        kernel,
        out_shape=out_shape,
        in_specs=specs or [VMEM] * len(operands),
        out_specs=outs or jax.tree.map(lambda _: VMEM, out_shape),
        scratch_shapes=list(scratch),
        compiler_params=pltpu.CompilerParams(vmem_limit_bytes=vmem * MIB),
        cost_estimate=pl.CostEstimate(flops=flops, bytes_accessed=0, transcendentals=0),
    )(*operands)


class Block:
    def __init__(self, nx, ny, nz, c, r, split=False):
        self.split = split
        self.nx, self.ny, self.nz, self.c, self.r = nx, ny, nz, c, r
        self.plane = ny * nz

    def parted(self):
        return Block(self.nx, self.ny, self.nz, self.c, self.r, True)

    def send_shapes(self):
        rows = self.nz * PAIR
        x = jax.ShapeDtypeStruct((self.ny, rows, self.r), BF)
        y = jax.ShapeDtypeStruct((self.nx, rows, self.r), BF)
        planes = [2, 2, self.nx - 2, self.nx - 2] if self.split else [self.nx] * 2
        z = [jax.ShapeDtypeStruct((n * self.ny // 2, 2 * PAIR, self.r), BF) for n in planes]
        return [x, x, y, y, *z]

    def z_buffers(self, x):
        return (6, 7) if self.split and 0 < x < self.nx - 1 else (4, 5)

    def slot(self, face, x, y, z):
        if face < 2:
            return (y, pl.ds(z * PAIR, PAIR))
        if face < 4:
            return (x, pl.ds(z * PAIR, PAIR))
        plane = {0: 0, self.nx - 1: 1}.get(x, x - 1) if self.split else x
        return (plane * (self.ny // 2) + y // 2, pl.ds((y % 2) * PAIR, PAIR))

    def halo_faces(self, x_side, y, z):
        faces = [] if x_side is None else [x_side]
        if y == 0:
            faces.append(2)
        if y == self.ny - 1:
            faces.append(3)
        if z == 0:
            faces.append(4)
        if z == self.nz - 1:
            faces.append(5)
        return faces

    def work(self, x, x_side):
        return [
            (x * self.plane + y * self.nz + z, y, z, self.halo_faces(x_side, y, z))
            for y in range(self.ny)
            for z in range(self.nz)
        ]

    def of_planes(self, planes):
        return [(e, x, y, z, faces) for x, side in planes for e, y, z, faces in self.work(x, side)]

    def two_at_once(self, visit):
        lax.fori_loop(0, self.nx // 2, lambda i, carry: (visit([2 * i, 2 * i + 1]), carry)[1], 0)

    def every_plane(self, visit):
        lax.fori_loop(0, self.nx, lambda x, carry: (visit(x), carry)[1], 0)

    def inner_planes(self):
        return [(x, None) for x in range(1, self.nx - 1)]

    def end_planes(self):
        return [(0, 0), (self.nx - 1, 1)]

    def near_local(self, face, x, y, z):
        dx, dy, dz = [(-1, 0, 0), (1, 0, 0), (0, -1, 0), (0, 1, 0), (0, 0, -1), (0, 0, 1)][face]
        return (x + 1 + dx) * self.plane + (y + dy) * self.nz + (z + dz), face ^ 1


def even(axis):
    return lax.rem(lax.axis_index(axis), 2) == 0


def pick(block, near, f, x, y, z):
    place = block.slot(f, x, y, z)
    if f < 2:
        return near[f][place]
    axis, buffers = ("gy", (2, 3)) if f < 4 else ("gz", block.z_buffers(x))
    first, second = (near[i][place] for i in buffers)
    return jnp.where(even(axis), *((first, second) if f % 2 else (second, first)))


def send_traces(block, work, values, bt, sends):
    traces = [mm(jnp.concatenate([bt[f] for f in w[4]], axis=0), a).astype(BF) for w, a in zip(work, values)]
    low = {}
    for (_, x, y, z, faces), t in zip(work, traces):
        for i, f in enumerate(faces):
            piece = t[i * PAD : i * PAD + PAIR]
            if f < 2:
                sends[f][block.slot(f, x, y, z)] = piece
                continue
            where = (2, z) if f < 4 else (4, y)
            if f % 2 == 0:
                low[where] = piece
                continue
            axis, buffers = ("gy", (2, 3)) if f < 4 else ("gz", block.z_buffers(x))
            first, second = (sends[i] for i in buffers)
            place, other = block.slot(f, x, y, z), low.pop(where)
            first[place] = jnp.where(even(axis), piece, other)
            second[place] = jnp.where(even(axis), other, piece)


def only(work, faces):
    return [(*w[:4], [f for f in w[4] if f in faces]) for w in work]


X, Y, Z = (0, 1), (2, 3), (4, 5)


def first_sends(block, warm_start, a, trace_basis, bt):
    width = trace_basis.shape[-1]
    half = block.ny

    def along_x(w_ref, b_ref, low_ref, high_ref, w_buf, b_buf, sems):
        copies = [
            pltpu.make_async_copy(b_ref.at[pl.ds(0, 2)], b_buf, sems.at[0]),
            pltpu.make_async_copy(w_ref.at[pl.ds(0, half)], w_buf.at[pl.ds(0, half)], sems.at[1]),
            pltpu.make_async_copy(
                w_ref.at[pl.ds((block.nx - 1) * half, half)], w_buf.at[pl.ds(half, half)], sems.at[2]
            ),
        ]
        for copy in copies:
            copy.start()
        rows = lax.broadcasted_iota(jnp.int32, (block.c, block.nz * block.c), 0)
        cols = lax.broadcasted_iota(jnp.int32, (block.c, block.nz * block.c), 1)
        spread = [(cols == block.nz * rows + z).astype(BF) for z in range(block.nz)]
        none = jnp.zeros((PAD - width, block.c), BF)
        copies[0].wait()
        basis = [jnp.concatenate([b_buf[side], none], axis=0) for side in range(2)]
        wide = [
            jnp.concatenate([mm(basis[side], spread[z]).astype(BF) for z in range(block.nz)], axis=0)
            for side in range(2)
        ]
        for side, out_ref in enumerate((low_ref, high_ref)):
            copies[1 + side].wait()
            columns = [w_buf[side * half + y].reshape(block.nz * block.c, block.r) for y in range(half)]
            traces = [mm(wide[side], column).astype(BF) for column in columns]
            for y, t in enumerate(traces):
                for z in range(block.nz):
                    out_ref[block.slot(side, 0, y, z)] = t[z * PAD : z * PAD + PAIR]

    def others(a_ref, bt_ref, *sends):
        def visit(planes):
            work = block.of_planes([(x, None) for x in planes])
            send_traces(block, work, [a_ref[w[0]] for w in work], bt_ref, (None, None) + sends)

        block.two_at_once(visit)

    nx, ny, nz, c, r = warm_start.shape
    columns = warm_start.transpose(0, 1, 3, 2, 4).reshape(nx * ny, c, nz, r)
    shapes = block.send_shapes()
    scratch = [
        pltpu.VMEM((2 * ny, c, nz, r), BF),
        pltpu.VMEM((2, width, c), BF),
        pltpu.SemaphoreType.DMA((3,)),
    ]
    raw = [pltpu.with_memory_space_constraint(v, pltpu.HBM) for v in (columns, trace_basis.transpose(0, 2, 1))]
    first = call(along_x, shapes[:2], raw, FIRST, scratch, [HBM, HBM])
    return [*first, *call(others, shapes[2:], [a, bt], SECOND)]


def one_hots(o_ref, e):
    own = o_ref[e]
    group, modes = own.shape
    index = jnp.concatenate([own + v * modes for v in range(VARS)], axis=1)
    rows = lax.broadcasted_iota(jnp.int32, (PAD, VARS * modes), 0)
    return [(rows == index[f : f + 1]).astype(BF) for f in range(group)]


def prepared(block, jacobian, orientation, bt):
    count, group, width, _ = jacobian.shape
    many = 8

    def kernel(j_ref, o_ref, bt_ref, jp_ref, p_ref, bc_ref, ball_ref):
        for f in range(group):
            basis = bt_ref[f].astype(F32).T.astype(BF)
            ball_ref[:, f * PAD : (f + 1) * PAD] = basis
            bc_ref[f] = jnp.concatenate([basis, jnp.zeros((block.c, LANES - PAD), BF)], axis=1)
        none = jnp.zeros((PAD - width, PAD), BF)
        rows = lax.broadcasted_iota(jnp.int32, (PAD, width), 0)
        eye = (rows == lax.broadcasted_iota(jnp.int32, (PAD, width), 1)).astype(BF)

        def elements(step, carry):
            places = [many * step + i for i in range(many)]
            turned = [one_hots(o_ref, e) for e in places]
            both = [
                [mm_t(jnp.concatenate([eye, j_ref[e, f]], axis=0), turn[f]).astype(BF) for f in range(group)]
                for e, turn in zip(places, turned)
            ]
            for e, values in zip(places, both):
                for f in range(group):
                    p_ref[e, f] = values[f][:PAD]
                    jp_ref[e, f, :width] = values[f][PAD:]
                    jp_ref[e, f, width:] = none
            return carry

        lax.fori_loop(0, count // many, elements, 0)

    shape = jax.ShapeDtypeStruct((count, group, PAD, PAD), BF)
    bc = jax.ShapeDtypeStruct((group, block.c, LANES), BF)
    ball = jax.ShapeDtypeStruct((block.c, group * PAD), BF)
    return call(kernel, [shape, shape, bc, ball], [jacobian, orientation, bt], PREP)


def fill_traces(block, a_ref, bt_ref, t_ref):
    nx, plane = block.nx, block.plane
    t_ref[0:plane, 1] = jnp.zeros((plane, PAD, block.r), BF)
    t_ref[(nx + 1) * plane : (nx + 2) * plane, 0] = jnp.zeros((plane, PAD, block.r), BF)
    every = bt_ref[...].reshape(6 * PAD, block.c)

    def traces(x):
        t = []
        for i in range(0, plane, 2):
            pair = jnp.concatenate([a_ref[x * plane + i], a_ref[x * plane + i + 1]], axis=1)
            both = mm(every, pair).astype(BF)
            t += [both[:, : block.r], both[:, block.r :]]
        for i in range(plane):
            for f in range(6):
                t_ref[(x + 1) * plane + i, f] = t[i][f * PAD : (f + 1) * PAD]

    block.every_plane(traces)


def local_faces(block, y, z):
    return [f for f in range(6) if f < 2 or f not in block.halo_faces(None, y, z)]


def widened(pieces):
    gap = jnp.zeros((LANES - PAD, pieces[0].shape[1]), BF)
    return jnp.concatenate([part for p in pieces for part in (p, gap)], axis=0)


def coupled(bc_ref, faces, fluxes):
    return mm(jnp.concatenate([bc_ref[f] for f in faces], axis=1), widened(fluxes))


def local_residual(block, a, source, jp, bt, ball, after):
    def kernel(a_ref, s_ref, j_ref, bt_ref, ball_ref, *refs):
        r_ref, t_ref = refs[len(after) :]
        fill_traces(block, a_ref, bt_ref, t_ref)
        none = jnp.zeros((PAD, block.r), BF)

        def near_fluxes(j_ref, e, x, y, z, faces):
            fluxes = []
            for i in range(0, len(faces), 2):
                some = faces[i : i + 2]
                near = jnp.concatenate([t_ref[block.near_local(f, x, y, z)] for f in some], axis=1)
                both = mm(jnp.concatenate([j_ref[e, f] for f in some], axis=0), near).astype(BF)
                for k in range(len(some)):
                    fluxes.append(both[k * PAD : (k + 1) * PAD, k * block.r : (k + 1) * block.r])
            return fluxes

        def planes(step, carry):
            work = [
                (e, x, y, z, local_faces(block, y, z))
                for x in (2 * step, 2 * step + 1)
                for e, y, z, _ in block.work(x, None)
            ]
            full = []
            for e, x, y, z, faces in work:
                fluxes = dict(zip(faces, near_fluxes(j_ref, e, x, y, z, faces)))
                full.append(jnp.concatenate([fluxes.get(f, none) for f in range(6)], axis=0))
            rest = []
            for i in range(0, len(work), 2):
                both = mm(ball_ref[...], jnp.concatenate(full[i : i + 2], axis=1))
                rest += [both[:, : block.r], both[:, block.r :]]
            for w, value in zip(work, rest):
                r_ref[w[0]] = s_ref[w[0]].astype(F32) - value
            return carry

        lax.fori_loop(0, block.nx // 2, planes, 0)

    count = block.nx * block.plane
    traces = pltpu.VMEM(((block.nx + 2) * block.plane, 6, PAD, block.r), BF)
    shape = jax.ShapeDtypeStruct((count, block.c, block.r), F32)
    operands = [a, source, jp, bt, ball, *after]
    return call(kernel, shape, operands, LOCAL, [traces], [VMEM] * 5 + [ANY] * len(after))


def z_then_y(parts):
    return [*parts[4:], *parts[2:4]]


def by_face(refs):
    return (None, None) + tuple(refs[2:4]) + tuple(refs[:2])


def z_fluxes(block, halos, jp, after):
    def kernel(first_ref, second_ref, j_ref, _, out_ref):
        near = [None] * 4 + [first_ref, second_ref]
        work = only(block.of_planes(block.end_planes()), Z)
        fluxes = [mm(j_ref[e, f[0], :, :PAIR], pick(block, near, f[0], x, y, z)).astype(BF) for e, x, y, z, f in work]
        for i, flux in enumerate(fluxes):
            out_ref[i] = flux

    shape = jax.ShapeDtypeStruct((2 * block.plane, PAD, block.r), BF)
    return call(kernel, shape, [*halos, jp, after], WAIT_Z, specs=[VMEM, VMEM, VMEM, ANY])


def x_fluxes(block, halos, jp, along_z=()):
    count = 2 * block.plane

    def kernel(low_ref, high_ref, j_ref, *refs):
        near = (low_ref, high_ref)
        work = only(block.of_planes(block.end_planes()), X)
        fluxes = [mm(j_ref[e, f[0], :, :PAIR], pick(block, near, f[0], x, y, z)).astype(BF) for e, x, y, z, f in work]
        for i, flux in enumerate(fluxes):
            refs[-1][i] = flux
        for ref in refs[:-1]:
            refs[-1][count:] = ref[...]

    shape = jax.ShapeDtypeStruct((count * (1 + len(along_z)), PAD, block.r), BF)
    return call(kernel, shape, [*halos, jp, *along_z], WAIT)


def finish_sweep(block, later, halos, residual, inverse, jp, bt, bc):
    def finish(work, ready, near, r_ref, v_ref, j_ref, bc_ref):
        def flux(i, e, x, y, z, f):
            if f in X:
                return ready[i]
            if ready is not None and block.split and f in Z:
                return ready[2 * block.plane + i]
            return mm(j_ref[e, f, :, :PAIR], pick(block, near, f, x, y, z)).astype(BF)

        fluxes = [[flux(i, e, x, y, z, f) for f in faces] for i, (e, x, y, z, faces) in enumerate(work)]
        rest = [(r_ref[w[0]] - coupled(bc_ref, w[4], flux)).astype(BF) for w, flux in zip(work, fluxes)]
        return [mm(v_ref[w[0]], value).astype(BF) for w, value in zip(work, rest)]

    first = X + Z if later.split else X

    def ends(*refs):
        count = 2 if block.split else 4
        ready, near, refs = refs[0], (None, None, *refs[1 : 1 + count]), refs[1 + count :]
        fixed, (bt_ref, a_ref, *sends) = refs[:4], refs[4:]
        work = block.of_planes(block.end_planes())
        values = finish(work, ready, near, *fixed)
        send_traces(later, only(work, first), values, bt_ref, [*sends[:2], None, None, *sends[2:]])
        for w, value in zip(work, values):
            a_ref[w[0]] = value

    def inner(*refs):
        done_ref, fixed, (bt_ref, a_ref, *sends) = refs[0], refs[5:9], refs[9:]
        near = (None, None, *refs[1:3], *((None, None) if block.split else ()), *refs[3:5])
        sends = [None, None, *sends[:2], *((None, None) if later.split else ()), *sends[2:]]
        work = block.of_planes(block.inner_planes())
        outer = [(*w, done_ref[w[0]]) for w in block.of_planes(block.end_planes())]
        values = finish(work, None, near, *fixed)
        passed = only(outer, [f for f in range(6) if f not in first])
        passed = [(w, o[5]) for w, o in zip(passed, outer) if w[4]]
        send_traces(later, work, values, bt_ref, sends)
        send_traces(later, [w for w, _ in passed], [v for _, v in passed], bt_ref, sends)
        for w, value in zip(work, values):
            a_ref[w[0]] = value
        for w in outer:
            a_ref[w[0]] = w[5]

    fixed = [residual, inverse, jp, bc, bt]
    shapes = later.send_shapes()
    whole = jax.ShapeDtypeStruct((block.nx * block.plane, block.c, block.r), BF)
    early = [z_fluxes(block, halos[4:6], jp, residual)] if block.split else []
    ready = x_fluxes(block, halos[:2], jp, early)
    z = [] if block.split else halos[4:]
    leaving = shapes[:2] + (shapes[4:6] if later.split else [])
    part, *lead = call(ends, [whole] + leaving, [ready, *halos[2:4], *z, *fixed], FIRST)
    operands = [part, *halos[2:4], *halos[-2:], *fixed]
    a, *rest = call(inner, [whole] + shapes[2:4] + shapes[-2:], operands, SECOND)
    return a, [*lead[:2], *rest[:2], *lead[2:], *rest[2:]]


def local_gradient(block, a, jp, p, bt, after):
    columns = a.reshape(block.nx * block.ny, block.nz, block.c, block.r).transpose(0, 2, 1, 3)

    def kernel(a_ref, w_ref, j_ref, p_ref, bt_ref, _, g_ref, out_ref, t_ref, sem):
        leave = pltpu.make_async_copy(w_ref, out_ref, sem)
        leave.start()
        fill_traces(block, a_ref, bt_ref, t_ref)

        def plane(x, carry):
            grads = []
            for e, y, z, _ in block.work(x, None):
                rows = [jnp.zeros((1, block.r), F32)] * 8
                for f in local_faces(block, y, z):
                    both = jnp.concatenate([j_ref[e, f], p_ref[e, f]], axis=0)
                    both = mm(both, t_ref[block.near_local(f, x, y, z)])
                    own = t_ref[e + block.plane, f].astype(F32)
                    rows[f] = jnp.sum((own - both[PAD:]) * both[:PAD], axis=0, keepdims=True)
                grads.append((e, jnp.concatenate(rows, axis=0)))
            for e, value in grads:
                g_ref[e] = value
            return carry

        lax.fori_loop(0, block.nx, plane, 0)
        leave.wait()

    count = block.nx * block.plane
    shapes = [jax.ShapeDtypeStruct((count, 8, block.r), F32), jax.ShapeDtypeStruct(columns.shape, BF)]
    scratch = [
        pltpu.VMEM(((block.nx + 2) * block.plane, 6, PAD, block.r), BF),
        pltpu.SemaphoreType.DMA(()),
    ]
    operands = [a, columns, jp, p, bt, after]
    return call(kernel, shapes, operands, LOCAL, scratch, [VMEM] * 5 + [ANY], outs=[VMEM, HBM])


def finish_gradient(block, halos, owns, inside, jp, p):
    def add(work, near, own, j_ref, p_ref, g_ref):
        total = []
        for e, x, y, z, faces in work:
            rows = [jnp.zeros((1, block.r), F32)] * 8
            for f in faces:
                both = jnp.concatenate([j_ref[e, f, :, :PAIR], p_ref[e, f, :, :PAIR]], axis=0)
                both = mm(both, pick(block, near, f, x, y, z))
                gap = pick(block, own, f, x, y, z).astype(F32) - both[PAD : PAD + PAIR]
                rows[f] = jnp.sum(gap * both[:PAIR], axis=0, keepdims=True)
            total.append(g_ref[e] + jnp.concatenate(rows, axis=0))
        return total

    def along_x(*refs):
        near, own, (j_ref, p_ref, g_ref, out_ref) = refs[:2], refs[2:4], refs[4:]

        for x, side in block.end_planes():
            work = [(e, x, y, z, [side]) for e, y, z, _ in block.work(x, None)]
            for w, value in zip(work, add(work, near, own, j_ref, p_ref, g_ref)):
                out_ref[w[0]] = value
        kept = slice(block.plane, (block.nx - 1) * block.plane)
        out_ref[kept] = g_ref[kept]

    def others(*refs):
        near, own, (j_ref, p_ref, g_ref, out_ref) = by_face(refs[:4]), by_face(refs[4:8]), refs[8:]

        def visit(planes):
            work = block.of_planes([(x, None) for x in planes])
            total = add(work, near, own, j_ref, p_ref, g_ref)
            for i in range(0, len(work), block.nz):
                _, x, y, _, _ = work[i]
                for f in range(6):
                    rows = [g[f : f + 1] for g in total[i : i + block.nz]]
                    out_ref[x * block.ny + y, f] = jnp.concatenate(rows, axis=0)

        block.two_at_once(visit)

    inside = call(along_x, inside, [*halos[:2], *owns[:2], jp, p, inside], WAIT)
    shape = jax.ShapeDtypeStruct((block.nx * block.ny, 6, block.nz, block.r), F32)
    return call(others, shape, [*z_then_y(halos), *z_then_y(owns), jp, p, inside], LOCAL)


def exchange(sends):
    count = lax.axis_size("gx")
    up = [(i, (i + 1) % count) for i in range(count)]
    halos = [lax.ppermute(sends[1], "gx", up), lax.ppermute(sends[0], "gx", [(j, i) for i, j in up])]
    for i, send in enumerate(sends[2:]):
        axis = "gy" if i < 2 else "gz"
        count = lax.axis_size(axis)
        pairs = [(j, (j + 1) % count) for j in range(i % 2, count if axis == "gy" else count - 1, 2)]
        halos.append(lax.ppermute(send, axis, pairs + [(k, j) for j, k in pairs]))
    return halos


def on_device(adjoint_source, warm_start, block_inverse, face_jacobian, trace_basis, orientation):
    nx, ny, nz, c, r = warm_start.shape
    count = nx * ny * nz
    width = trace_basis.shape[-1]
    modes = orientation.shape[-1]
    block = Block(nx, ny, nz, c, r)
    gap = PAD - width

    bt = jnp.pad(trace_basis.transpose(0, 2, 1), ((0, 0), (0, gap), (0, 0)))
    adjoint = warm_start.reshape(count, c, r)
    sends = first_sends(block, warm_start, adjoint, trace_basis, bt)

    source = adjoint_source.reshape(count, c, r)
    inverse = block_inverse.reshape(count, c, c)
    turns = orientation.reshape(count, 6, modes)
    jacobian = face_jacobian.reshape(count, 6, width, width)
    jp, p, bc, ball = prepared(block, jacobian, turns, bt)

    parted = block.parted()
    for sweep in range(SWEEPS):
        halos = exchange(sends)
        now, later = (block, parted) if sweep == 0 else (parted, block)
        after = [halos[0] if sweep == 0 else halos[4]]
        residual = local_residual(block, adjoint, source, jp, bt, ball, after)
        if sweep == 0:
            inverse, residual = lax.optimization_barrier((block_inverse, residual))
            inverse = inverse.reshape(count, c, c)
        adjoint, sends = finish_sweep(now, later, halos, residual, inverse, jp, bt, bc)
    halos = exchange(sends)
    inside, adjoint = local_gradient(block, adjoint, jp, p, bt, halos[0])
    adjoint = adjoint.reshape(nx, ny, c, nz, r).transpose(0, 1, 3, 2, 4)
    gradient = finish_gradient(block, halos, sends, inside, jp, p)
    gradient = gradient.reshape(nx, ny, 6, nz, r).transpose(0, 1, 3, 2, 4)
    return (adjoint, gradient)


def solution(mesh):
    return jax.shard_map(
        on_device,
        mesh=mesh,
        in_specs=(
            P("gx", "gy", "gz", None, None),
            P("gx", "gy", "gz", None, None),
            P("gx", "gy", "gz", None, None),
            P("gx", "gy", "gz", None, None, None),
            P(),
            P("gx", "gy", "gz", None, None),
        ),
        out_specs=(P("gx", "gy", "gz", None, None), P("gx", "gy", "gz", None, None)),
        check_vma=False,
    )
```
